32 devices in a mesh: dp: 16 (over z, y, x), tensor: 2 (over core).
Axes of the slice: x: 2, y: 2, z: 4, core: 2. Of those that a mesh axis runs over, the one named last changes fastest.
Arguments:
- inputs: bfloat16 [4096, 768], P('dp'), may hold values from -6 to 6
- lengths: int32 [32], P('dp'), may hold values from 1 to 128, as said below
- w_qkv: bfloat16 [2, 3, 768, 768], P(None, None, None, 'tensor'), may hold values from -0.21875 to 0.21875
- w_out: bfloat16 [2, 768, 768], P(None, 'tensor'), may hold values from -0.875 to 0.875
- w_in: bfloat16 [2, 2, 768, 3072], P(None, None, None, 'tensor'), may hold values from -0.21875 to 0.21875
- w_down: bfloat16 [2, 3072, 768], P(None, 'tensor'), may hold values from -0.15625 to 0.15625
- norm_gain: float32 [2, 2, 768], replicated, may hold values from 0.5 to 1.5
- norm_bias: float32 [2, 2, 768], replicated, may hold values from -3 to 3
- cotangent: bfloat16 [4096, 768], P('dp'), may hold values from -6 to 6
Outputs:
- encoded: bfloat16 [4096, 768], P('dp')
- input_grad: float32 [4096, 768], P('dp')
- grad_w_qkv: float32 [2, 3, 768, 768], P(None, None, 'dp', 'tensor')
- grad_w_out: float32 [2, 768, 768], P(None, 'tensor', 'dp')
- grad_w_in: float32 [2, 2, 768, 3072], P(None, None, 'dp', 'tensor')
- grad_w_down: float32 [2, 3072, 768], P(None, 'tensor', 'dp')
- grad_norm_gain: float32 [2, 2, 768], P(None, None, 'dp')
- grad_norm_bias: float32 [2, 2, 768], P(None, None, 'dp')
The draws below stay inside these ranges and needn't reach their ends.
Inputs may be any that keep to these rules, and one draw needn't show every extreme that they name: `lengths`: among each run of 2 windows that starts at a multiple of 2, at least one has all 128 slots live.
All inputs are finite; a program needn't handle non-finite values.
Results may differ from the reference program's by a relative error of at most 0.025.
Values sent between devices are 32-bit elements; how exact they have to be, the bound alone decides.
A program may use at most 192 MiB of HBM per device.

```python
import jax
import jax.numpy as jnp
from jax import lax

D = 768
HEADS = 12
FF = 3072
HEAD_DIM = 64
LEN = 128
LAYERS = 2
WIN_DEV = 2
WINDOWS = 32
TOKENS = 4096


def draw_lengths(key, part):
    key = jax.random.fold_in(key, 7)
    first_key, second_key = jax.random.split(key)
    random_picks = jax.random.randint(first_key, (WINDOWS,), 0, LEN)
    window_lengths = 1 + random_picks * random_picks // LEN
    full_choice = jax.random.randint(second_key, (WINDOWS // WIN_DEV,), 0, WIN_DEV)
    slot_index = jnp.arange(WINDOWS, dtype=jnp.int32) % WIN_DEV
    full_slot = jnp.repeat(full_choice, WIN_DEV)
    return jnp.where(slot_index == full_slot, LEN, window_lengths).astype(jnp.int32)


def raised(drawn, rng, source, target, shards_of, factor):
    owner, partner = [(jnp.arange(drawn.shape[dim]) // (drawn.shape[dim] // shards_of)).reshape([-1 if axis == dim else 1 for axis in range(drawn.ndim)]) for dim in (source, target)]
    chosen = jax.random.permutation(rng, shards_of)[partner]
    strong = (owner == chosen) | (owner == (partner + shards_of // 2) % shards_of)
    return jnp.where(strong, factor * drawn, drawn)


def levels(rng, shape, cuts, smallest, high):
    def one(dim, parts):
        heights = jax.random.uniform(jax.random.fold_in(jax.random.fold_in(rng, 6), dim), (parts,), jnp.float32, smallest / len(cuts), high / len(cuts))
        return jnp.repeat(jnp.exp(heights), shape[dim] // parts).reshape((-1,) + (1,) * (len(shape) - dim - 1))

    factor_of = one(*cuts[0])
    for cut in cuts[1:]:
        factor_of = factor_of * one(*cut)
    return factor_of


def normal_values(own_key, extent, scale, most, pieces=(), kind=jnp.bfloat16):
    factor_of = levels(own_key, extent, pieces, -0.22, 0.18) if pieces else 1.0
    values = jax.random.normal(own_key, extent, jnp.float32) * scale * factor_of
    return jnp.minimum(jnp.maximum(values, -most), most).astype(kind)


def bell_draw_with(stream_key, extent, scale, most, cuts, heavy, kind=jnp.bfloat16):
    drawn = scale * jax.random.normal(stream_key, extent, jnp.float32)
    if cuts:
        drawn = drawn * levels(stream_key, extent, cuts, -0.22, 0.18)
    return jnp.clip(raised(drawn, jax.random.fold_in(stream_key, 3), *heavy), -most, most).astype(kind)


def setup_inputs(seed: int = 0) -> dict:
    streams_of = jax.random.split(jax.random.key(seed), 10)
    return {
        "inputs": normal_values(streams_of[0], (TOKENS, D), 1.0, 6.0, ((0, 16),)),
        "lengths": draw_lengths(jax.random.fold_in(streams_of[9], 71), 0),
        "w_qkv": normal_values(streams_of[2], (LAYERS, 3, D, D), D ** -0.5, 0.21875, ((3, 2),)),
        "w_out": normal_values(streams_of[3], (LAYERS, D, D), (D // 16) ** -0.5, 0.875, ((1, 2),)),
        "w_in": normal_values(streams_of[4], (LAYERS, 2, D, FF), D ** -0.5, 0.21875, ((3, 2),)),
        "w_down": normal_values(streams_of[5], (LAYERS, FF, D), (FF // 2) ** -0.5, 0.15625, ((1, 2),)),
        "norm_gain": jnp.clip(1.0 + 0.1 * jax.random.normal(streams_of[6], (LAYERS, 2, D), jnp.float32), 0.5, 1.5),
        "norm_bias": normal_values(streams_of[7], (LAYERS, 2, D), 0.5, 3.0, (), jnp.float32),
        "cotangent": bell_draw_with(streams_of[8], (TOKENS, D), 1.0, 6.0, ((0, 16),), (0, 1, 16, 2.0)),
    }


@jax.custom_vjp
def low(v):
    return lax.optimization_barrier(v.astype(jnp.bfloat16)).astype(jnp.float32)

@jax.custom_vjp
def low_back(v):
    return v

def low_keep(v):
    return (low(v), None)

def low_pass(kept, grad):
    return (grad,)

def back_keep(v):
    return (v, None)

def back_low(kept, grad):
    return (low(grad),)
low.defvjp(low_keep, low_pass)
low_back.defvjp(back_keep, back_low)
EPS = 1e-05
MASKED = -1000000000.0
HIGH = lax.Precision.HIGHEST

def normalize(values, gain_vec, shift_vec):
    center = values - lax.optimization_barrier(jnp.mean(values, -1, keepdims=True))
    spread = lax.optimization_barrier(jnp.mean(center * center, -1, keepdims=True))
    return center * lax.rsqrt(spread + EPS) * gain_vec + shift_vec

def alibi_table():
    head_order = jnp.arange(HEADS, dtype=jnp.int32).astype(jnp.float32)
    slopes = 2.0 ** (-8.0 * (head_order + 1.0) / HEADS)
    places = jnp.arange(LEN, dtype=jnp.int32)
    distance = jnp.abs(places[:, None] - places[None, :]).astype(jnp.float32)
    return -slopes[:, None, None] * distance

def tensor_sum(left_side, right_side):
    total = jnp.einsum('glk,kd->gld', left_side, right_side, precision=HIGH)
    return low_back(total)

def encoder_layer(layer_rows, qkv_weight, out_weight, in_weight, down_weight, gains_now, shifts_now, key_live, bias_table):
    groups = layer_rows.shape[0]
    rows_low = low(layer_rows)
    projected = low(low_back(jnp.einsum('gld,cde->cgle', rows_low, qkv_weight, precision=HIGH)))
    heads_split = projected.reshape(3, groups, LEN, HEADS, HEAD_DIM)
    raw_scores = jnp.einsum('gqhe,gkhe->ghqk', heads_split[0], heads_split[1], precision=HIGH) * HEAD_DIM ** (-0.5) + bias_table[None]
    scores = jnp.where(key_live[:, None, None, :], low_back(raw_scores), MASKED)
    probabilities = low(jax.nn.softmax(scores, axis=-1))
    mixed_heads = jnp.einsum('ghqk,gkhe->gqhe', probabilities, heads_split[2], precision=HIGH).reshape(groups, LEN, D)
    mixed_heads = low(low_back(mixed_heads))
    hidden = layer_rows + tensor_sum(mixed_heads, out_weight)
    normed = normalize(hidden, gains_now[0], shifts_now[0])
    gate_up = low_back(jnp.einsum('gld,cdf->cglf', low(normed), in_weight, precision=HIGH))
    gated = low(jax.nn.gelu(gate_up[0], approximate=False) * gate_up[1])
    summed = normed + tensor_sum(gated, down_weight)
    return normalize(summed, gains_now[1], shifts_now[1])

def reference(inputs, lengths, w_qkv, w_out, w_in, w_down, norm_gain, norm_bias, cotangent):
    weights = (w_qkv.astype(jnp.float32), w_out.astype(jnp.float32), w_in.astype(jnp.float32), w_down.astype(jnp.float32), norm_gain.astype(jnp.float32), norm_bias.astype(jnp.float32))
    blocks = WINDOWS // 16
    row_blocks = inputs.astype(jnp.float32).reshape(blocks, 16, LEN, D)
    cot_blocks = cotangent.astype(jnp.float32).reshape(blocks, 16, LEN, D)
    live_blocks = jnp.arange(LEN, dtype=jnp.int32)[None, None, :] < lengths.astype(jnp.int32).reshape(blocks, 16)[:, :, None]
    bias_table = alibi_table()

    def one_block(totals, item):
        block_rows, block_cot, key_live = item

        def forward(layer_rows, qkv_all, out_all, in_all, down_all, gain_all, shift_all):
            for layer_index in range(LAYERS):
                layer_rows = encoder_layer(layer_rows, qkv_all[layer_index], out_all[layer_index], in_all[layer_index], down_all[layer_index], gain_all[layer_index], shift_all[layer_index], key_live, bias_table)
            return layer_rows
        output, pull = jax.vjp(forward, block_rows, weights[0], weights[1], weights[2], weights[3], weights[4], weights[5])
        grads = pull(block_cot)
        totals = tuple((total + grad for total, grad in zip(totals, grads[1:])))
        return (totals, (output, grads[0]))
    zeros = tuple((jnp.zeros(weight.shape, jnp.float32) for weight in weights))
    totals, (outputs, input_grads) = lax.scan(one_block, zeros, (row_blocks, cot_blocks, live_blocks))
    return (outputs.reshape(TOKENS, D).astype(jnp.bfloat16), input_grads.reshape(TOKENS, D), totals[0], totals[1], totals[2], totals[3], totals[4], totals[5])
```

```python
import functools

import jax
import jax.numpy as jnp
from jax import lax
from jax.experimental import pallas as pl
from jax.experimental.pallas import tpu as pltpu
from jax.sharding import PartitionSpec as P

HEADS = 12
HEAD_DIM = 64
EPS = 1e-05
MASKED = -1000000000.0
MESH = pl.DeviceIdType.MESH
F32 = jnp.float32
BF16 = jnp.bfloat16
PLANE = 4
DP = 16


def dot(a, b):
    return lax.dot_general(a, b, (((1,), (0,)), ((), ())), preferred_element_type=F32)


def dot_t(a, b):
    return lax.dot_general(a, b, (((1,), (1,)), ((), ())), preferred_element_type=F32)


def dot_tt(a, b):
    return lax.dot_general(a, b, (((0,), (0,)), ((), ())), preferred_element_type=F32)


def gelu_parts(g):
    bell = jnp.exp(-0.5 * g * g)
    d = 1.0 + (0.3275911 * 0.7071067811865476) * jnp.abs(g)
    t = pl.reciprocal(d, approx=True)
    t = t * (2.0 - d * t)
    poly = t * (0.127414796 + t * (-0.142248368 + t * (0.7107068705 + t * (-0.7265760135 + t * 0.5307027145))))
    tail = poly * bell
    phi = jnp.where(g >= 0, 1.0 - tail, tail)
    return g * phi, phi + g * (bell * 0.3989422804014327)


def kernel(
    T, D, E, F, L,
    len_ref, x_ref, cot_ref, gain_ref, bias_ref, wq_hbm, wo_hbm, wi_hbm, wd_hbm,
    enc_ref, igrad_ref, oatt, offn, gn, ag,
    wq, wo, wi, wd, xb, qkv, pb, om, hhat, zhat, hr, zr, xcur, acur, ab, psend, precv, eb, AB, dob, dqkv, xbT, dabT,
    abT, dfbT, edg, stage, GS, RZ1, RZ2, GA, RA1, RA2, RA3, RA4, gnr,
    wsem, ps_s, ps_r, agl, ag_s, ag_r, stsem, fz_s, fz_r, fa_s, fa_r, fl, at_s, at_r, atl, gn_s, gn_r, cr_att, cr_ffn,
):
    dp = lax.axis_index("dp")
    c = lax.axis_index("tensor")
    q = lax.rem(dp, PLANE)
    x = lax.rem(dp, 2)
    y = lax.rem(lax.div(dp, 2), 2)
    z0 = lax.rem(lax.div(dp, 4), 2)
    z1 = lax.div(dp, 8)
    nx, ny, nz0, nz1 = 1 - x, 1 - y, 1 - z0, 1 - z1
    sib = (dp, 1 - c)
    px = (dp + 1 - 2 * x, c)
    py = (dp + 2 - 4 * y, c)
    pxy = (dp + 3 - 2 * x - 4 * y, c)
    pz0 = (dp + 4 - 8 * z0, c)
    pz1 = (dp + 8 - 16 * z1, c)
    W = T // 128
    NP = E // 128
    FQ = F // PLANE
    NC = D // 256
    R = D // DP
    RB = D // (DP // PLANE)

    barrier = pltpu.get_barrier_semaphore()
    for peer in (sib, px, py, pxy, pz0, pz1):
        pl.semaphore_signal(barrier, inc=1, device_id=peer, device_id_type=MESH)
    pl.semaphore_wait(barrier, 6)

    def remote(src, dst, ss, rs, peer):
        return pltpu.make_async_remote_copy(
            src_ref=src, dst_ref=dst, send_sem=ss, recv_sem=rs, device_id=peer, device_id_type=MESH
        )

    wcopies = {}
    for l in range(L):
        for i, (src, dst) in enumerate(((wq_hbm, wq), (wo_hbm, wo), (wi_hbm, wi), (wd_hbm, wd))):
            cp = pltpu.make_async_copy(src.at[l], dst.at[l], wsem.at[l, i])
            cp.start()
            wcopies[l, i] = cp

    RC = 64
    row_chunks = [pl.ds(r, RC) for r in range(0, T, RC)]

    def psum_send(slot, part):
        cps = []
        for n in range(NC):
            psend[slot, n] = part(n)
            cp = remote(psend.at[slot, n], precv.at[slot, n], ps_s.at[slot, n], ps_r.at[slot, n], sib)
            cp.start()
            cps.append(cp)
        return cps

    def psum_wait(cps):
        for cp in cps:
            cp.wait()

    def psum_rows(slot, rows):
        return jnp.concatenate([psend[slot, n, rows, :] + precv[slot, n, rows, :] for n in range(NC)], axis=1)

    def norm_rows(v):
        center = v - jnp.mean(v, -1, keepdims=True)
        r = lax.rsqrt(jnp.mean(center * center, -1, keepdims=True) + EPS)
        return center * r, r

    def ln_bwd_rows(dy, hat, r, gain):
        t = dy * gain
        m1 = jnp.mean(t, -1, keepdims=True)
        m2 = jnp.mean(t * hat, -1, keepdims=True)
        return r * (t - m1 - hat * m2)

    lane = lax.broadcasted_iota(jnp.int32, (128, 128), 1)
    first = lane < HEAD_DIM

    def halves(v):
        zero = jnp.zeros_like(v)
        return jnp.concatenate([jnp.where(first, v, zero), jnp.where(first, zero, v)], axis=0)

    def ag_local(k):
        cp = pltpu.make_async_copy(acur, ag.at[k, q], agl.at[k])
        cp.start()
        return cp

    def ag_send(k, local):
        local.wait()
        cps = []
        for j, peer in enumerate((px, py, pxy)):
            cp = remote(ag.at[k, q], ag.at[k, q], ag_s.at[k, j], ag_r.at[k, j], peer)
            cp.start()
            cps.append(cp)
        return cps

    slope_table = [[2.0 ** (-8.0 * (cc * (E // HEAD_DIM) + h + 1.0) / HEADS) for h in range(E // HEAD_DIM)] for cc in range(HEADS * HEAD_DIM // E)]

    def slope(h):
        s = jnp.float32(slope_table[0][h])
        for cc in range(1, len(slope_table)):
            s = jnp.where(c == cc, jnp.float32(slope_table[cc][h]), s)
        return s

    def forward(l, src_rows):
        for rows in row_chunks:
            xb[l, rows, :] = src_rows(rows).astype(BF16)
        wcopies[l, 0].wait()
        for k in range(3):
            qkv[l, k] = dot(xb[l], wq[l, k]).astype(BF16)
        dist = jnp.abs(
            lax.broadcasted_iota(jnp.int32, (128, 128), 0) - lane
        ).astype(F32)

        def attend(w, _):
            rows = pl.ds(pl.multiple_of(w * 128, 128), 128)
            live = lane < len_ref[w]
            for p in range(NP):
                cols = pl.ds(p * 128, 128)
                kk = halves(qkv[l, 1, rows, cols])
                vv = halves(qkv[l, 2, rows, cols])
                s = dot_t(qkv[l, 0, rows, cols], kk)
                both = []
                for i in range(2):
                    si = s[:, i * 128:(i + 1) * 128] * (HEAD_DIM ** -0.5) - slope(2 * p + i) * dist
                    si = jnp.where(live, si, MASKED)
                    ei = jnp.exp(si - jnp.max(si, -1, keepdims=True))
                    both.append(ei / jnp.sum(ei, -1, keepdims=True))
                prob = jnp.concatenate(both, axis=1).astype(BF16)
                pb[l, w, p] = prob
                om[l, rows, cols] = dot(prob, vv).astype(BF16)
            return 0

        lax.fori_loop(0, W, attend, 0)
        wcopies[l, 1].wait()
        cps = psum_send(0, lambda n: dot(om[l], wo[l, :, pl.ds(n * 256, 256)]))
        wcopies[l, 2].wait()
        psum_wait(cps)
        gain, bias = gain_ref[l, 0:1, :], bias_ref[l, 0:1, :]
        for rows in row_chunks:
            hat, r = norm_rows(src_rows(rows) + psum_rows(0, rows))
            hhat[l, rows, :] = hat.astype(BF16)
            hr[l, rows, :] = r
            a = hat * gain + bias
            acur[rows, :] = a
            ab[rows, :] = a.astype(BF16)
        local = ag_local(l)

        def hidden(j, _):
            cols = pl.ds(pl.multiple_of(j * 256, 256), 256)
            g = dot(ab[...], wi[l, 0, :, cols])
            u = dot(ab[...], wi[l, 1, :, cols])
            act, slope_g = gelu_parts(g)
            eb[:, cols] = (act * u).astype(BF16)
            AB[l, 0, :, cols] = act.astype(BF16)
            AB[l, 1, :, cols] = (slope_g * u).astype(BF16)
            return 0

        lax.fori_loop(0, F // 256, hidden, 0)
        sends = ag_send(l, local)
        wcopies[l, 3].wait()
        cps = psum_send(1, lambda n: dot(eb[...], wd[l, :, pl.ds(n * 256, 256)]))
        psum_wait(cps)
        gain, bias = gain_ref[l, 1:2, :], bias_ref[l, 1:2, :]
        for rows in row_chunks:
            hat, r = norm_rows(acur[rows, :] + psum_rows(1, rows))
            zhat[l, rows, :] = hat.astype(BF16)
            zr[l, rows, :] = r
            out = hat * gain + bias
            if l == L - 1:
                enc_ref[rows, :] = out.astype(BF16)
            else:
                xcur[rows, :] = out
        return sends

    def bwd_norm2(l, src_rows):
        gain = gain_ref[l, 1:2, :]
        dg = jnp.zeros((1, D), F32)
        db = jnp.zeros((1, D), F32)
        for rows in row_chunks:
            dy = src_rows(rows)
            hat = zhat[l, rows, :].astype(F32)
            dz = ln_bwd_rows(dy, hat, zr[l, rows, :], gain)
            acur[rows, :] = dz
            ab[rows, :] = dz.astype(BF16)
            dg = dg + jnp.sum(dy * hat, 0, keepdims=True)
            db = db + jnp.sum(dy, 0, keepdims=True)
        gn[pl.ds(2 * l + 1, 1), :] = dg
        gn[pl.ds(2 * L + 2 * l + 1, 1), :] = db

    def bwd_hidden(l):
        def hidden(j, _):
            cols = pl.ds(pl.multiple_of(j * 256, 256), 256)
            de = dot_t(ab[...], wd[l, cols, :])
            dg = de * AB[l, 1, :, cols].astype(F32)
            du = de * AB[l, 0, :, cols].astype(F32)
            AB[l, 0, :, cols] = dg.astype(BF16)
            AB[l, 1, :, cols] = du.astype(BF16)
            return 0

        lax.fori_loop(0, F // 256, hidden, 0)

    def bwd_ffn_sum(l):
        return psum_send(
            0,
            lambda n: dot_t(AB[l, 0], wi[l, 0, pl.ds(n * 256, 256), :]) + dot_t(AB[l, 1], wi[l, 1, pl.ds(n * 256, 256), :]),
        )

    def bwd_norm1(l):
        gain = gain_ref[l, 0:1, :]
        dg = jnp.zeros((1, D), F32)
        db = jnp.zeros((1, D), F32)
        for rows in row_chunks:
            da = acur[rows, :] + psum_rows(0, rows)
            hat = hhat[l, rows, :].astype(F32)
            dh = ln_bwd_rows(da, hat, hr[l, rows, :], gain)
            acur[rows, :] = dh
            ab[rows, :] = dh.astype(BF16)
            dg = dg + jnp.sum(da * hat, 0, keepdims=True)
            db = db + jnp.sum(da, 0, keepdims=True)
        gn[pl.ds(2 * l, 1), :] = dg
        gn[pl.ds(2 * L + 2 * l, 1), :] = db

    def bwd_attention(l):
        dob[...] = dot_t(ab[...], wo[l]).astype(BF16)

        def attend(w, _):
            rows = pl.ds(pl.multiple_of(w * 128, 128), 128)
            for p in range(NP):
                cols = pl.ds(p * 128, 128)
                qq = qkv[l, 0, rows, cols]
                kk = halves(qkv[l, 1, rows, cols])
                vv = halves(qkv[l, 2, rows, cols])
                do = dob[rows, cols]
                prob = pb[l, w, p]
                dprob = dot_t(do, vv)
                p32 = prob.astype(F32)
                both = []
                for i in range(2):
                    pi, di = p32[:, i * 128:(i + 1) * 128], dprob[:, i * 128:(i + 1) * 128]
                    both.append(pi * (di - jnp.sum(pi * di, -1, keepdims=True)))
                ds = jnp.concatenate(both, axis=1).astype(BF16)
                dv2 = dot_tt(prob, do)
                dk2 = dot_tt(ds, qq)
                scale = HEAD_DIM ** -0.5
                dqkv[0, rows, cols] = (dot(ds, kk) * scale).astype(BF16)
                dqkv[1, rows, cols] = (jnp.where(first, dk2[:128], dk2[128:]) * scale).astype(BF16)
                dqkv[2, rows, cols] = jnp.where(first, dv2[:128], dv2[128:]).astype(BF16)
            return 0

        lax.fori_loop(0, W, attend, 0)

    def bwd_qkv_sum(l):
        return psum_send(
            1,
            lambda n: sum(dot_t(dqkv[k], wq[l, k, pl.ds(n * 256, 256), :]) for k in range(3)),
        )

    def att_views(k):
        if k < 2:
            return (
                (GA.at[k, :, :, :, nx], GA.at[k, :, :, :, x], RA1.at[k], px),
                (GA.at[k, :, :, ny, x], GA.at[k, :, :, y, x], RA2.at[k], py),
                (GA.at[k, :, nz0, y, x], GA.at[k, :, z0, y, x], RA3.at[k], pz0),
                (GA.at[k, nz1, z0, y, x], GA.at[k, z1, z0, y, x], RA4.at[k], pz1),
            )
        return (
            (GA.at[k, :, :, ny], GA.at[k, :, :, y], RA1.at[k], py),
            (GA.at[k, :, :, y, nx], GA.at[k, :, :, y, x], RA2.at[k], px),
            (GA.at[k, :, nz0, y, x], GA.at[k, :, z0, y, x], RA3.at[k], pz0),
            (GA.at[k, nz1, z0, y, x], GA.at[k, z1, z0, y, x], RA4.at[k], pz1),
        )

    att_cp = {}

    def att_send(l, k, step):
        src, _, dst, peer = att_views(k)[step]
        if l < L - 1:
            pl.semaphore_wait(cr_att.at[k, step], 1)
        cp = remote(src, dst, at_s.at[k, step], at_r.at[k, step], peer)
        cp.start()
        att_cp[l, k, step] = cp

    def att_recv(l, k, step):
        _, keep, dst, peer = att_views(k)[step]
        att_cp[l, k, step].wait_recv()
        keep[...] = keep[...] + dst[...]
        if l > 0:
            pl.semaphore_signal(cr_att.at[k, step], inc=1, device_id=peer, device_id_type=MESH)
        if step < 3:
            att_send(l, k, step + 1)
        else:
            cp = pltpu.make_async_copy(GA.at[k, z1, z0, y, x], oatt.at[l, k], atl.at[k])
            cp.start()
            att_cp[l, k, "out"] = cp

    def att_done(l, k):
        for step in range(4):
            att_cp[l, k, step].wait_send()
        att_cp[l, k, "out"].wait()

    def att_grad_prepare(l):
        xbT[...] = xb[l].T
        dabT[...] = ab[...].T

    def att_grad(l, k):
        left, right = (xbT, dqkv.at[k]) if k < 3 else (dabT, om.at[l])
        for i in range(2):
            half = D // 2
            GA[k, i] = dot(left[pl.ds(i * half, half), :], right[...]).reshape(2, 2, 2, R, E)
        att_send(l, k, 0)

    def stage_copies(l, src, slot):
        return (
            pltpu.make_async_copy(ag.at[l, src], stage.at[slot, 0], stsem.at[slot, 0]),
            pltpu.make_async_copy(ag.at[2 * L - 1 - l, src], stage.at[slot, 1], stsem.at[slot, 1]),
        )

    def ffn_hidden(l):
        for cp in stage_copies(l, 0, 0):
            cp.start()
        qcols = pl.ds(pl.multiple_of(q * FQ, 128), FQ)

        def chunk(s, _):
            slot = lax.rem(s, 2)

            @pl.when(s < PLANE - 1)
            def _():
                for cp in stage_copies(l, s + 1, 1 - slot):
                    cp.start()

            for cp in stage_copies(l, s, slot):
                cp.wait()
            toks = pl.ds(pl.multiple_of(s * T, T), T)
            a = stage[slot, 0].astype(BF16)
            dfb = stage[slot, 1].astype(BF16)
            abT[:, toks] = a.T
            dfbT[:, toks] = dfb.T
            g = dot(a, wi[l, 0, :, qcols])
            u = dot(a, wi[l, 1, :, qcols])
            de = dot_t(dfb, wd[l, qcols, :])
            act, slope_g = gelu_parts(g)
            edg[toks, pl.ds(0, FQ)] = (de * u * slope_g).astype(BF16)
            edg[toks, pl.ds(FQ, FQ)] = (de * act).astype(BF16)
            edg[toks, pl.ds(2 * FQ, FQ)] = (act * u).astype(BF16)
            return 0

        lax.fori_loop(0, PLANE, chunk, 0)

    ffn_cp = {}

    def ffn_block(l, i):
        b1, b0 = ((nz1, nz0), (z1, nz0), (nz1, z0), (z1, z0))[i]
        rows = pl.ds(pl.multiple_of((b1 * 2 + b0) * RB, 64), RB)
        for k in range(3):
            left = abT if k < 2 else dfbT
            GS[b1, b0, k] = dot(left[rows, :], edg[:, pl.ds(k * FQ, FQ)])
        if i < 2:
            if l < L - 1:
                pl.semaphore_wait(cr_ffn.at[i], 1)
            cp = remote(GS.at[b1, b0], RZ1.at[i], fz_s.at[i], fz_r.at[i], pz0)
            cp.start()
            ffn_cp[l, i] = cp

    def ffn_recv(l, i):
        b1 = (nz1, z1)[i]
        ffn_cp[l, i].wait_recv()
        for k in range(3):
            GS[b1, z0, k] = GS[b1, z0, k] + RZ1[i, k]
        if l > 0:
            pl.semaphore_signal(cr_ffn.at[i], inc=1, device_id=pz0, device_id_type=MESH)
        if i == 0:
            if l < L - 1:
                pl.semaphore_wait(cr_ffn.at[2], 1)
            cp = remote(GS.at[nz1, z0], RZ2, fz_s.at[2], fz_r.at[2], pz1)
            cp.start()
            ffn_cp[l, 2] = cp

    def ffn_last(l):
        ffn_cp[l, 2].wait_recv()
        for k in range(3):
            GS[z1, z0, k] = GS[z1, z0, k] + RZ2[k]
        if l > 0:
            pl.semaphore_signal(cr_ffn.at[2], inc=1, device_id=pz1, device_id_type=MESH)
        out_cols = pl.ds(pl.multiple_of(q * FQ, 128), FQ)

        def rows_of(xx, yy):
            return GS.at[z1, z0, :, pl.ds(pl.multiple_of((yy * 2 + xx) * R, 16), R), :]

        cps = []
        for j, (xx, yy, peer) in enumerate(((nx, y, px), (x, ny, py), (nx, ny, pxy))):
            cp = remote(rows_of(xx, yy), offn.at[l, :, :, out_cols], fa_s.at[l, j], fa_r.at[l, j], peer)
            cp.start()
            cps.append(cp)
        own = pltpu.make_async_copy(rows_of(x, y), offn.at[l, :, :, out_cols], fl.at[l])
        own.start()
        ffn_cp[l, 3] = (cps, own)

    def ffn_sent(l):
        for i in range(3):
            ffn_cp[l, i].wait_send()
        cps, own = ffn_cp[l, 3]
        for cp in cps:
            cp.wait_send()
        own.wait()

    def ffn_arrived(l):
        for cp in ffn_cp[l, 3][0]:
            cp.wait_recv()

    def gn_step(step):
        peer = (px, py, pz0, pz1)[step]
        cp = remote(gn, gnr.at[step], gn_s.at[step], gn_r.at[step], peer)
        cp.start()
        cp.wait()
        gn[...] = gn[...] + gnr[step]

    def x_in(rows):
        return x_ref[rows, :].astype(F32)

    def x_now(rows):
        return xcur[rows, :]

    def cot_in(rows):
        return cot_ref[rows, :].astype(F32)

    ag_cp = {}
    for l in range(L):
        ag_cp[l] = forward(l, x_in if l == 0 else x_now)

    dy_rows = cot_in
    bwd_norm2(L - 1, dy_rows)
    local = ag_local(L)
    for l in reversed(range(L)):
        k = 2 * L - 1 - l
        bwd_hidden(l)
        if l == L - 1:
            ag_cp[k] = ag_send(k, local)
        cps = bwd_ffn_sum(l)
        if l < L - 1:
            for kk in range(4):
                att_recv(l + 1, kk, 0)
        psum_wait(cps)
        bwd_norm1(l)
        bwd_attention(l)
        cps = bwd_qkv_sum(l)
        att_grad_prepare(l)
        if l < L - 1:
            ffn_recv(l + 1, 0)
            for kk in range(4):
                att_recv(l + 1, kk, 1)
            ffn_recv(l + 1, 1)
            for kk in range(4):
                att_recv(l + 1, kk, 2)
            ffn_last(l + 1)
            for kk in range(4):
                att_recv(l + 1, kk, 3)
            for kk in range(4):
                att_done(l + 1, kk)
        for kk in range(4):
            att_grad(l, kk)
        psum_wait(cps)
        for rows in row_chunks:
            dx = acur[rows, :] + psum_rows(1, rows)
            if l == 0:
                igrad_ref[rows, :] = dx
            else:
                xcur[rows, :] = dx
        if l > 0:
            bwd_norm2(l - 1, x_now)
            local = ag_local(k + 1)
            ag_cp[k + 1] = ag_send(k + 1, local)
        if l < L - 1:
            ffn_sent(l + 1)
        for kk in (l, k):
            for cp in ag_cp[kk]:
                cp.wait()
        ffn_hidden(l)
        for i in range(4):
            ffn_block(l, i)

    for step in range(4):
        gn_step(step)
    ffn_recv(0, 0)
    for kk in range(4):
        att_recv(0, kk, 0)
    for kk in range(4):
        att_recv(0, kk, 1)
    ffn_recv(0, 1)
    for kk in range(4):
        att_recv(0, kk, 2)
    ffn_last(0)
    for kk in range(4):
        att_recv(0, kk, 3)
    for kk in range(4):
        att_done(0, kk)
    ffn_sent(0)
    for l in range(L):
        ffn_arrived(l)


def fused(inputs, lengths, w_qkv, w_out, w_in, w_down, norm_gain, norm_bias, cotangent):
    T, D = inputs.shape
    L, _, _, E = w_qkv.shape
    F = w_in.shape[-1]
    W, NP, NC, FQ = T // 128, E // 128, D // 256, F // PLANE
    R, RB = D // DP, D // (DP // PLANE)
    vmem = pl.BlockSpec(memory_space=pltpu.VMEM)
    smem = pl.BlockSpec(memory_space=pltpu.SMEM)
    hbm = pl.BlockSpec(memory_space=pl.ANY)
    V = pltpu.VMEM
    DMA = pltpu.SemaphoreType.DMA
    REG = pltpu.SemaphoreType.REGULAR
    scratch = [
        V((L, 3, D, E), BF16), V((L, E, D), BF16), V((L, 2, D, F), BF16), V((L, F, D), BF16),
        V((L, T, D), BF16), V((L, 3, T, E), BF16), V((L, W, NP, 128, 256), BF16), V((L, T, E), BF16),
        V((L, T, D), BF16), V((L, T, D), BF16), V((L, T, 1), F32), V((L, T, 1), F32),
        V((T, D), F32), V((T, D), F32), V((T, D), BF16),
        V((2, NC, T, 256), F32), V((2, NC, T, 256), F32),
        V((T, F), BF16), V((L, 2, T, F), BF16), V((T, E), BF16), V((3, T, E), BF16),
        V((D, T), BF16), V((D, T), BF16),
        V((D, PLANE * T), BF16), V((D, PLANE * T), BF16), V((PLANE * T, 3 * FQ), BF16),
        V((2, 2, T, D), F32),
        V((2, 2, 3, RB, FQ), F32), V((2, 3, RB, FQ), F32), V((3, RB, FQ), F32),
        V((4, 2, 2, 2, 2, R, E), F32), V((4, 2, 2, 2, R, E), F32), V((4, 2, 2, R, E), F32),
        V((4, 2, R, E), F32), V((4, R, E), F32),
        V((4, 4 * L, D), F32),
        DMA((L, 4)), DMA((2, NC)), DMA((2, NC)), DMA((2 * L,)), DMA((2 * L, 3)), DMA((2 * L, 3)), DMA((2, 2)),
        DMA((3,)), DMA((3,)), DMA((L, 3)), DMA((L, 3)), DMA((L,)), DMA((4, 4)), DMA((4, 4)), DMA((4,)),
        DMA((4,)), DMA((4,)), REG((4, 4)), REG((3,)),
    ]
    outs = pl.pallas_call(
        functools.partial(kernel, T, D, E, F, L),
        out_shape=(
            jax.ShapeDtypeStruct((T, D), BF16),
            jax.ShapeDtypeStruct((T, D), F32),
            jax.ShapeDtypeStruct((L, 4, R, E), F32),
            jax.ShapeDtypeStruct((L, 3, R, F), F32),
            jax.ShapeDtypeStruct((4 * L, D), F32),
            jax.ShapeDtypeStruct((2 * L, PLANE, T, D), F32),
        ),
        in_specs=[smem, vmem, vmem, vmem, vmem, hbm, hbm, hbm, hbm],
        out_specs=(vmem, vmem, hbm, hbm, vmem, hbm),
        scratch_shapes=scratch,
        compiler_params=pltpu.CompilerParams(collective_id=0, has_side_effects=True, vmem_limit_bytes=63 * 2**20),
        name="encoder",
    )(lengths, inputs, cotangent, norm_gain, norm_bias, w_qkv, w_out, w_in, w_down)
    encoded, input_grad, oatt, offn, gn, _ = outs
    mine = lax.dynamic_slice_in_dim(gn.reshape(2, L, 2, D), lax.axis_index("dp") * R, R, axis=3)
    return (
        encoded,
        input_grad,
        oatt[:, :3],
        jnp.swapaxes(oatt[:, 3], 1, 2),
        offn[:, :2],
        jnp.swapaxes(offn[:, 2], 1, 2),
        mine[0],
        mine[1],
    )


def normalize(values, gain_vec, shift_vec):
    center = values - jnp.mean(values, -1, keepdims=True)
    spread = jnp.mean(center * center, -1, keepdims=True)
    return center * lax.rsqrt(spread + EPS) * gain_vec + shift_vec


def gating(gate_pre, up_pre):
    return jax.nn.gelu(gate_pre, approximate=False) * up_pre


def head_bias(heads_local, length):
    first_head = lax.axis_index("tensor") * heads_local
    head_order = (first_head + jnp.arange(heads_local, dtype=jnp.int32)).astype(jnp.float32)
    slopes = 2.0 ** (-8.0 * (head_order + 1.0) / HEADS)
    places = jnp.arange(length, dtype=jnp.int32)
    distance = jnp.abs(places[:, None] - places[None, :]).astype(jnp.float32)
    return -slopes[:, None, None] * distance


def scores_of(query_heads, key_heads, bias_table, key_live):
    score_scale = query_heads.shape[-1] ** (-0.5)
    raw_scores = (
        jnp.einsum("wqhe,wkhe->whqk", query_heads, key_heads, preferred_element_type=jnp.float32)
        * score_scale
        + bias_table[None]
    )
    return jnp.where(key_live[:, None, None, :], raw_scores, MASKED)


def layer_forward(layer_rows, params, bias_table, key_live):
    qkv_weight, out_weight, in_weight, down_weight, gains_now, shifts_now = params
    windows, length = key_live.shape
    heads_local = bias_table.shape[0]
    rows_low = layer_rows.astype(jnp.bfloat16)
    projected = jnp.einsum(
        "td,cde->cte", rows_low, qkv_weight, preferred_element_type=jnp.float32
    ).astype(jnp.bfloat16)
    heads_split = projected.reshape(3, windows, length, heads_local, HEAD_DIM)
    scores = scores_of(heads_split[0], heads_split[1], bias_table, key_live)
    row_max = jnp.max(scores, -1, keepdims=True)
    log_total = row_max + jnp.log(jnp.sum(jnp.exp(scores - row_max), -1, keepdims=True))
    weights_low = jnp.exp(scores - log_total).astype(jnp.bfloat16)
    mixed_heads = jnp.einsum(
        "whqk,wkhe->wqhe", weights_low, heads_split[2], preferred_element_type=jnp.float32
    )
    mixed_heads = mixed_heads.astype(jnp.bfloat16).reshape(windows * length, heads_local * HEAD_DIM)
    attended = lax.psum(
        jnp.dot(mixed_heads, out_weight, preferred_element_type=jnp.float32), "tensor"
    )
    hidden = layer_rows + attended
    normed = normalize(hidden, gains_now[0], shifts_now[0])
    normed_low = normed.astype(jnp.bfloat16)
    gate_up = jnp.einsum("td,cdf->ctf", normed_low, in_weight, preferred_element_type=jnp.float32)
    gated_low = gating(gate_up[0], gate_up[1]).astype(jnp.bfloat16)
    fed_back = lax.psum(
        jnp.dot(gated_low, down_weight, preferred_element_type=jnp.float32), "tensor"
    )
    summed = normed + fed_back
    output = normalize(summed, gains_now[1], shifts_now[1])
    stored = (
        rows_low,
        projected,
        log_total,
        mixed_heads,
        hidden,
        normed_low,
        gate_up,
        gated_low,
        summed,
    )
    return (output, stored)


def layer_backward(grad_output, stored, params, bias_table, key_live):
    rows_low, projected, log_total, mixed_heads, hidden, normed_low, gate_up, gated_low, summed = (
        stored
    )
    qkv_weight, out_weight, in_weight, down_weight, gains_now, shifts_now = params
    windows, length = key_live.shape
    heads_local = bias_table.shape[0]
    _, pull_second = jax.vjp(normalize, summed, gains_now[1], shifts_now[1])
    grad_summed, gain_second, shift_second = pull_second(grad_output)
    grad_fed = grad_summed.astype(jnp.bfloat16)
    grad_gated = jnp.einsum("td,fd->tf", grad_fed, down_weight, preferred_element_type=jnp.float32)
    grad_down = jnp.einsum("tf,td->fd", gated_low, grad_fed, preferred_element_type=jnp.float32)
    _, pull_gate = jax.vjp(gating, gate_up[0], gate_up[1])
    grad_gate_pre, grad_up_pre = pull_gate(grad_gated)
    grad_gate_up = jnp.stack([grad_gate_pre, grad_up_pre]).astype(jnp.bfloat16)
    ffn_back = lax.psum(
        jnp.einsum("ctf,cdf->td", grad_gate_up, in_weight, preferred_element_type=jnp.float32),
        "tensor",
    )
    grad_in = jnp.einsum(
        "td,ctf->cdf", normed_low, grad_gate_up, preferred_element_type=jnp.float32
    )
    grad_normed = grad_summed + ffn_back
    _, pull_first = jax.vjp(normalize, hidden, gains_now[0], shifts_now[0])
    grad_hidden, gain_first, shift_first = pull_first(grad_normed)
    grad_attended = grad_hidden.astype(jnp.bfloat16)
    grad_mixed = jnp.einsum(
        "td,ed->te", grad_attended, out_weight, preferred_element_type=jnp.float32
    ).astype(jnp.bfloat16)
    grad_out_proj = jnp.einsum(
        "te,td->ed", mixed_heads, grad_attended, preferred_element_type=jnp.float32
    )
    heads_split = projected.reshape(3, windows, length, heads_local, HEAD_DIM)
    scores = scores_of(heads_split[0], heads_split[1], bias_table, key_live)
    probabilities = jnp.exp(scores - log_total)
    probs_low = probabilities.astype(jnp.bfloat16)
    grad_heads = grad_mixed.reshape(windows, length, heads_local, HEAD_DIM)
    grad_probs = jnp.einsum(
        "wqhe,wkhe->whqk", grad_heads, heads_split[2], preferred_element_type=jnp.float32
    )
    grad_values = jnp.einsum(
        "whqk,wqhe->wkhe", probs_low, grad_heads, preferred_element_type=jnp.float32
    )
    row_dot = jnp.sum(probabilities * grad_probs, -1, keepdims=True)
    grad_scores = (probabilities * (grad_probs - row_dot)).astype(jnp.bfloat16)
    score_scale = HEAD_DIM ** (-0.5)
    grad_query = (
        jnp.einsum(
            "whqk,wkhe->wqhe", grad_scores, heads_split[1], preferred_element_type=jnp.float32
        )
        * score_scale
    )
    grad_keys = (
        jnp.einsum(
            "whqk,wqhe->wkhe", grad_scores, heads_split[0], preferred_element_type=jnp.float32
        )
        * score_scale
    )
    grad_projected = jnp.stack([grad_query, grad_keys, grad_values]).astype(jnp.bfloat16)
    grad_projected = grad_projected.reshape(3, windows * length, heads_local * HEAD_DIM)
    attn_back = lax.psum(
        jnp.einsum("cte,cde->td", grad_projected, qkv_weight, preferred_element_type=jnp.float32),
        "tensor",
    )
    grad_qkv = jnp.einsum(
        "td,cte->cde", rows_low, grad_projected, preferred_element_type=jnp.float32
    )
    grad_rows = grad_hidden + attn_back
    grad_gains = jnp.stack([gain_first, gain_second])
    grad_shifts = jnp.stack([shift_first, shift_second])
    return (grad_rows, (grad_qkv, grad_out_proj, grad_in, grad_down, grad_gains, grad_shifts))


def body(inputs, lengths, w_qkv, w_out, w_in, w_down, norm_gain, norm_bias, cotangent):
    windows = lengths.shape[0]
    length = inputs.shape[0] // windows
    heads_local = w_qkv.shape[-1] // HEAD_DIM
    bias_table = head_bias(heads_local, length)
    key_live = jnp.arange(length, dtype=jnp.int32)[None, :] < lengths[:, None]
    layers = w_qkv.shape[0]
    layer_rows = inputs.astype(jnp.float32)
    stored_all = []
    for layer_index in range(layers):
        params = (
            w_qkv[layer_index],
            w_out[layer_index],
            w_in[layer_index],
            w_down[layer_index],
            norm_gain[layer_index],
            norm_bias[layer_index],
        )
        layer_rows, stored = layer_forward(layer_rows, params, bias_table, key_live)
        stored_all.append(stored)
    encoded = layer_rows.astype(jnp.bfloat16)
    grad_rows = cotangent.astype(jnp.float32)
    pieces = [None] * layers
    for layer_index in reversed(range(layers)):
        params = (
            w_qkv[layer_index],
            w_out[layer_index],
            w_in[layer_index],
            w_down[layer_index],
            norm_gain[layer_index],
            norm_bias[layer_index],
        )
        grad_rows, layer_grads = layer_backward(
            grad_rows, stored_all[layer_index], params, bias_table, key_live
        )
        pieces[layer_index] = layer_grads
    stacked = [jnp.stack([pieces[index][member] for index in range(layers)]) for member in range(6)]
    stacked = (
        lax.psum_scatter(stacked[0], "dp", scatter_dimension=2, tiled=True),
        lax.psum_scatter(stacked[1], "dp", scatter_dimension=2, tiled=True),
        lax.psum_scatter(stacked[2], "dp", scatter_dimension=2, tiled=True),
        lax.psum_scatter(stacked[3], "dp", scatter_dimension=2, tiled=True),
        lax.psum_scatter(stacked[4], "dp", scatter_dimension=2, tiled=True),
        lax.psum_scatter(stacked[5], "dp", scatter_dimension=2, tiled=True),
    )
    return (
        encoded,
        grad_rows,
        stacked[0],
        stacked[1],
        stacked[2],
        stacked[3],
        stacked[4],
        stacked[5],
    )


def solution(mesh):
    return jax.shard_map(
        fused if mesh.shape["dp"] == DP and mesh.shape["tensor"] == 2 else body,
        mesh=mesh,
        in_specs=(
            P("dp", None),
            P("dp"),
            P(None, None, None, "tensor"),
            P(None, "tensor", None),
            P(None, None, None, "tensor"),
            P(None, "tensor", None),
            P(),
            P(),
            P("dp", None),
        ),
        out_specs=(
            P("dp", None),
            P("dp", None),
            P(None, None, "dp", "tensor"),
            P(None, "tensor", "dp"),
            P(None, None, "dp", "tensor"),
            P(None, "tensor", "dp"),
            P(None, None, "dp"),
            P(None, None, "dp"),
        ),
        check_vma=False,
    )
```

```python
import functools

import jax
import jax.numpy as jnp
from jax import lax
from jax.experimental import pallas as pl
from jax.experimental.pallas import tpu as pltpu
from jax.sharding import PartitionSpec as P

HEADS = 12
HEAD_DIM = 64
EPS = 1e-05
MASKED = -1000000000.0
MESH = pl.DeviceIdType.MESH
F32 = jnp.float32
BF16 = jnp.bfloat16
GROUP = 4
DP = 16
AXES = ("z1", "z0", "y", "x")
SHARE = (("z1", "y"), ("z0", "x"))
FFN = ((("x", "z0"), ("z0", "x")), (("y", "z1"), ("z1", "y")))
PAIR = ("z0", "y")
ATT = ((("y", "x", "z1"), ("y", "x", "z1")), (("z0", "z1", "x"), ("x", "z0", "z1")))


def dot(a, b):
    return lax.dot_general(a, b, (((1,), (0,)), ((), ())), preferred_element_type=F32)


def dot_t(a, b):
    return lax.dot_general(a, b, (((1,), (1,)), ((), ())), preferred_element_type=F32)


def dot_tt(a, b):
    return lax.dot_general(a, b, (((0,), (0,)), ((), ())), preferred_element_type=F32)


def gelu_parts(g):
    bell = jnp.exp(-0.5 * g * g)
    d = 1.0 + (0.3275911 * 0.7071067811865476) * jnp.abs(g)
    t = pl.reciprocal(d, approx=True)
    t = t * (2.0 - d * t)
    poly = t * (0.127414796 + t * (-0.142248368 + t * (0.7107068705 + t * (-0.7265760135 + t * 0.5307027145))))
    tail = poly * bell
    phi = jnp.where(g >= 0, 1.0 - tail, tail)
    return g * phi, phi + g * (bell * 0.3989422804014327)


def kernel(
    T, D, E, F, L,
    len_ref, x_hbm, cot_hbm, gain_ref, bias_ref, wq_hbm, wo_hbm, wi_hbm, wd_hbm,
    enc_ref, igrad_ref, oatt, offn, gn, ag, az,
    wq, wo, wi, wd, xb, qkv, pb, om, hhat, zhat, hr, zr, xcur, acur, ab, psend, precv, eb, AB,
    LT, LA, abT, dfbT, wab, wdfb, lens, GF, RF1, RF2, GA, RA1, RA2, RA3, gnr,
    wsem, insem, ps_s, ps_r, agl, aga_s, aga_r, agb_s, agb_r, agf_s, agf_r, agc_s, agc_r,
    ln_s, ln_r, igl, azl, azz_s, azz_r, azc_s, azc_r, stsem, fz_s, fz_r, fa_s, fa_r, fl, at_s, at_r, ato_s, ato_r, atl, gn_s, gn_r,
):
    dp = lax.axis_index("dp")
    c = lax.axis_index("tensor")
    weight = {"x": 1, "y": 2, "z0": 4, "z1": 8}
    me = {a: lax.rem(lax.div(dp, w), 2) for a, w in weight.items()}
    other = {a: 1 - me[a] for a in AXES}

    def peer(*axes):
        return (dp + sum(weight[a] * (1 - 2 * me[a]) for a in axes), c)

    sib = (dp, 1 - c)
    W = T // 128
    NP = E // 128
    FQ = F // GROUP
    NC = D // 256
    R = D // DP
    HT = T // 2
    QL = E

    barrier = pltpu.get_barrier_semaphore()
    friends = [sib] + [peer(a) for a in AXES] + [peer(*p) for p in sorted(set(SHARE))]
    for friend in friends:
        pl.semaphore_signal(barrier, inc=1, device_id=friend, device_id_type=MESH)
    pl.semaphore_wait(barrier, len(friends))

    def remote(src, dst, ss, rs, to):
        cp = pltpu.make_async_remote_copy(
            src_ref=src, dst_ref=dst, send_sem=ss, recv_sem=rs, device_id=to, device_id_type=MESH
        )
        cp.start()
        return cp

    def here(src, dst, sem):
        cp = pltpu.make_async_copy(src, dst, sem)
        cp.start()
        return cp

    wcopies = {}
    x_cp = here(x_hbm, ab, insem.at[0])
    for l in range(L):
        for i, (src, dst) in enumerate(((wq_hbm, wq), (wo_hbm, wo), (wi_hbm, wi), (wd_hbm, wd))):
            wcopies[l, i] = here(src.at[l], dst.at[l], wsem.at[l, i])

    RC = 64
    row_chunks = [pl.ds(r, RC) for r in range(0, T, RC)]

    def psum_send(slot, part):
        cps = []
        for n in range(NC):
            cols = pl.ds(n * 256, 256)
            psend[slot, :, cols] = part(n)
            cps.append(remote(psend.at[slot, :, cols], precv.at[slot, :, cols], ps_s.at[slot, n], ps_r.at[slot, n], sib))
        return cps

    def psum_wait(cps):
        for cp in cps:
            cp.wait()

    def psum_rows(slot, rows):
        return psend[slot, rows, :] + precv[slot, rows, :]

    def norm_rows(v):
        center = v - jnp.mean(v, -1, keepdims=True)
        r = lax.rsqrt(jnp.mean(center * center, -1, keepdims=True) + EPS)
        return center * r, r

    def ln_bwd_rows(dy, hat, r, gain):
        t = dy * gain
        m1 = jnp.mean(t, -1, keepdims=True)
        m2 = jnp.mean(t * hat, -1, keepdims=True)
        return r * (t - m1 - hat * m2)

    half = pl.ds(pl.multiple_of(c * HT, 128), HT)

    class Group:
        def __init__(self, k):
            A, B = SHARE[min(k, 2 * L - 1 - k)]
            self.k, self.A, self.B = k, A, B
            self.slots = {"own": (me[A], me[B]), "A": (other[A], me[B]), "B": (me[A], other[B]), "AB": (other[A], other[B])}

        def slot(self, name):
            i, j = self.slots[name]
            return ag.at[self.k, i, j]

        def keep(self, src):
            self.own = here(src, self.slot("own"), agl.at[self.k])

        def send(self, src=None):
            k = self.k
            mine = self.slot("own").at[half]
            if src is None:
                self.own.wait()
                src = mine
            else:
                src = src.at[half]
            self.ac = remote(src, mine, aga_s.at[k], aga_r.at[k], peer(self.A))
            self.bc = remote(src, mine, agb_s.at[k], agb_r.at[k], peer(self.B))

        def forward(self):
            k = self.k
            self.ac.wait_recv()
            ref = self.slot("A").at[half]
            self.fc = remote(ref, ref, agf_s.at[k], agf_r.at[k], peer(self.B))

        def share(self):
            k = self.k
            self.bc.wait_recv()
            self.fc.wait_recv()
            self.cc = []
            for j, name in enumerate(("A", "B", "AB")):
                ref = self.slot(name).at[half]
                self.cc.append(remote(ref, ref, agc_s.at[k, j], agc_r.at[k, j], sib))

        def sent(self):
            self.ac.wait_send()
            self.bc.wait_send()

        def ready(self):
            for cp in self.cc:
                cp.wait()
            self.fc.wait_send()

    class Pair:
        def __init__(self, k):
            self.k, self.axis = k, PAIR[min(k, 2 * L - 1 - k)]

        def keep(self, src):
            self.own = here(src, az.at[self.k, me[self.axis]], azl.at[self.k])

        def send(self):
            k = self.k
            self.own.wait()
            mine = az.at[k, me[self.axis], half]
            self.zc = remote(mine, mine, azz_s.at[k], azz_r.at[k], peer(self.axis))

        def share(self):
            k = self.k
            self.zc.wait()
            ref = az.at[k, other[self.axis], half]
            self.cc = remote(ref, ref, azc_s.at[k], azc_r.at[k], sib)

        def ready(self):
            self.cc.wait()

    for w in range(W):
        lens[0, pl.ds(w, 1), :] = jnp.full((1, 128), len_ref[w], jnp.int32).astype(F32)
    len_cp = [remote(lens.at[0], lens.at[1 + l], ln_s.at[l], ln_r.at[l], peer(PAIR[l])) for l in range(L)]

    def dfb_index(l):
        return 2 * L - 1 - l

    groups = [Group(k) for k in range(2 * L)]
    pairs = [Pair(k) for k in range(2 * L)]

    lane = lax.broadcasted_iota(jnp.int32, (128, 128), 1)
    first = lane < HEAD_DIM
    dist = jnp.abs(lax.broadcasted_iota(jnp.int32, (128, 128), 0) - lane).astype(F32)
    scale = HEAD_DIM ** -0.5

    def halves(v):
        zero = jnp.zeros_like(v)
        return jnp.concatenate([jnp.where(first, v, zero), jnp.where(first, zero, v)], axis=0)

    def pick(table, index):
        s = jnp.float32(table[0])
        for i in range(1, len(table)):
            s = jnp.where(index == i, jnp.float32(table[i]), s)
        return s

    heads_local = E // HEAD_DIM
    slopes = [2.0 ** (-8.0 * (h + 1.0) / HEADS) for h in range(HEADS)]

    def slope(h):
        return pick(slopes[h::heads_local], c)

    def slope_outer(i, side):
        table = []
        for cc in range(HEADS // heads_local):
            table += [slopes[cc * heads_local + i], slopes[cc * heads_local + 2 * (NP - 1) + i]]
        return pick(table, 2 * c + side)

    def attend(qq, kk, vv, live, slope_pair):
        s = dot_t(qq, kk)
        both = []
        for i in range(2):
            si = s[:, i * 128:(i + 1) * 128] * scale - slope_pair[i] * dist
            si = jnp.where(live, si, MASKED)
            ei = jnp.exp(si - jnp.max(si, -1, keepdims=True))
            both.append(ei * (1.0 / jnp.sum(ei, -1, keepdims=True)))
        prob = jnp.concatenate(both, axis=1).astype(BF16)
        return prob, dot(prob, vv).astype(BF16)

    def attend_bwd(qq, kk, vv, prob, do):
        dprob = dot_t(do, vv)
        p32 = prob.astype(F32)
        both = []
        for i in range(2):
            pi, di = p32[:, i * 128:(i + 1) * 128], dprob[:, i * 128:(i + 1) * 128]
            both.append(pi * (di - jnp.sum(pi * di, -1, keepdims=True)))
        ds = jnp.concatenate(both, axis=1).astype(BF16)
        dv2 = dot_tt(prob, do)
        dk2 = dot_tt(ds, qq)
        dq = (dot(ds, kk) * scale).astype(BF16)
        dk = (jnp.where(first, dk2[:128], dk2[128:]) * scale).astype(BF16)
        dv = jnp.where(first, dv2[:128], dv2[128:]).astype(BF16)
        return dq, dk, dv

    def nothing():
        pass

    def fwd_attention(l, mid=nothing):
        pairs[l].keep(xcur)
        for rows in row_chunks:
            xb[l, rows, :] = xcur[rows, :].astype(BF16)
        wcopies[l, 0].wait()
        for k in range(3):
            qkv[l, k] = dot(xb[l], wq[l, k]).astype(BF16)
        pairs[l].send()
        mid()

        def window(w, _):
            rows = pl.ds(pl.multiple_of(w * 128, 128), 128)
            live = lane < len_ref[w]
            for p in range(NP):
                cols = pl.ds(p * 128, 128)
                kk, vv = halves(qkv[l, 1, rows, cols]), halves(qkv[l, 2, rows, cols])
                prob, out = attend(qkv[l, 0, rows, cols], kk, vv, live, (slope(2 * p), slope(2 * p + 1)))
                pb[l, w, p] = prob
                om[l, rows, cols] = out
            return 0

        lax.fori_loop(0, W, window, 0)
        wcopies[l, 1].wait()
        return psum_send(0, lambda n: dot(om[l], wo[l, :, pl.ds(n * 256, 256)]))

    def fwd_norm1(l, cps):
        psum_wait(cps)
        gain, bias = gain_ref[l, 0:1, :], bias_ref[l, 0:1, :]
        for rows in row_chunks:
            hat, r = norm_rows(xcur[rows, :] + psum_rows(0, rows))
            hhat[l, rows, :] = hat.astype(BF16)
            hr[l, rows, :] = r
            a = hat * gain + bias
            acur[rows, :] = a
            ab[rows, :] = a.astype(BF16)
        groups[l].keep(acur)

    def fwd_ffn(l, mid=nothing):
        wcopies[l, 2].wait()

        def hidden(j, _):
            cols = pl.ds(pl.multiple_of(j * 256, 256), 256)
            g = dot(ab[...], wi[l, 0, :, cols])
            u = dot(ab[...], wi[l, 1, :, cols])
            act, slope_g = gelu_parts(g)
            eb[:, cols] = (act * u).astype(BF16)
            AB[l, 0, :, cols] = act.astype(BF16)
            AB[l, 1, :, cols] = (slope_g * u).astype(BF16)
            return 0

        lax.fori_loop(0, 2, hidden, 0)
        groups[l].send()
        lax.fori_loop(2, F // 256, hidden, 0)
        mid()
        wcopies[l, 3].wait()
        return psum_send(1, lambda n: dot(eb[...], wd[l, :, pl.ds(n * 256, 256)]))

    def fwd_norm2(l, cps):
        psum_wait(cps)
        gain, bias = gain_ref[l, 1:2, :], bias_ref[l, 1:2, :]
        for rows in row_chunks:
            hat, r = norm_rows(acur[rows, :] + psum_rows(1, rows))
            zhat[l, rows, :] = hat.astype(BF16)
            zr[l, rows, :] = r
            out = hat * gain + bias
            if l == L - 1:
                enc_ref[rows, :] = out.astype(BF16)
            else:
                xcur[rows, :] = out

    def bwd_norm2(l, dy_rows):
        gain = gain_ref[l, 1:2, :]
        dg = jnp.zeros((1, D), F32)
        db = jnp.zeros((1, D), F32)
        for rows in row_chunks:
            dy = dy_rows(rows)
            hat = zhat[l, rows, :].astype(F32)
            dz = ln_bwd_rows(dy, hat, zr[l, rows, :], gain)
            acur[rows, :] = dz
            ab[rows, :] = dz.astype(BF16)
            dg = dg + jnp.sum(dy * hat, 0, keepdims=True)
            db = db + jnp.sum(dy, 0, keepdims=True)
        gn[pl.ds(2 * l + 1, 1), :] = dg
        gn[pl.ds(2 * L + 2 * l + 1, 1), :] = db
        groups[dfb_index(l)].send(acur)
        groups[dfb_index(l)].keep(acur)

    def bwd_ffn(l, mid=nothing):
        def hidden(j, _):
            cols = pl.ds(pl.multiple_of(j * 256, 256), 256)
            de = dot_t(ab[...], wd[l, cols, :])
            dg = de * AB[l, 1, :, cols].astype(F32)
            du = de * AB[l, 0, :, cols].astype(F32)
            AB[l, 0, :, cols] = dg.astype(BF16)
            AB[l, 1, :, cols] = du.astype(BF16)
            return 0

        lax.fori_loop(0, F // 256, hidden, 0)
        mid()
        return psum_send(
            0,
            lambda n: dot_t(AB[l, 0], wi[l, 0, pl.ds(n * 256, 256), :]) + dot_t(AB[l, 1], wi[l, 1, pl.ds(n * 256, 256), :]),
        )

    def bwd_norm1(l, cps):
        psum_wait(cps)
        gain = gain_ref[l, 0:1, :]
        dg = jnp.zeros((1, D), F32)
        db = jnp.zeros((1, D), F32)
        for rows in row_chunks:
            da = acur[rows, :] + psum_rows(0, rows)
            hat = hhat[l, rows, :].astype(F32)
            dh = ln_bwd_rows(da, hat, hr[l, rows, :], gain)
            xcur[rows, :] = dh
            ab[rows, :] = dh.astype(BF16)
            dg = dg + jnp.sum(da * hat, 0, keepdims=True)
            db = db + jnp.sum(da, 0, keepdims=True)
        gn[pl.ds(2 * l, 1), :] = dg
        gn[pl.ds(2 * L + 2 * l, 1), :] = db
        pairs[dfb_index(l)].keep(xcur)

    def dqkv(k):
        return pl.ds(k * QL, QL)

    def bwd_attention(l, mid=nothing, late=nothing):
        eb[:, dqkv(3)] = dot_t(ab[...], wo[l]).astype(BF16)
        pairs[dfb_index(l)].send()
        mid()

        def window(w, _):
            rows = pl.ds(pl.multiple_of(w * 128, 128), 128)
            for p in range(NP):
                cols = pl.ds(p * 128, 128)
                kk, vv = halves(qkv[l, 1, rows, cols]), halves(qkv[l, 2, rows, cols])
                grads = attend_bwd(qkv[l, 0, rows, cols], kk, vv, pb[l, w, p], eb[rows, pl.ds(3 * QL + p * 128, 128)])
                for k in range(3):
                    eb[rows, pl.ds(k * QL + p * 128, 128)] = grads[k]
            return 0

        lax.fori_loop(0, W, window, 0)
        late()
        return psum_send(
            1,
            lambda n: sum(dot_t(eb[:, dqkv(k)], wq[l, k, pl.ds(n * 256, 256), :]) for k in range(3)),
        )

    def bwd_input(l, cps):
        psum_wait(cps)
        for rows in row_chunks:
            dx = xcur[rows, :] + psum_rows(1, rows)
            xcur[rows, :] = dx

    middle = 128

    def side_of(l):
        side = me[PAIR[l]]
        return side, pl.multiple_of(side * (E - 128), 128)

    def att_own(l):
        side, outer = side_of(l)
        own = pl.ds(0, T)
        LT[0, :, own] = xb[l].T
        LT[1, :, own] = ab[...].T
        for k in range(3):
            LA[own, pl.ds(k * 128, 128)] = eb[:, pl.ds(pl.multiple_of(k * QL + outer, 128), 128)]
        LA[own, pl.ds(3 * 128, 128)] = om[l, :, pl.ds(outer, 128)]
        low = side == 0
        LA[own, pl.ds(4 * 128, 128)] = jnp.where(low, eb[:, pl.ds(middle, 128)], eb[:, pl.ds(2 * QL + middle, 128)])
        LA[own, pl.ds(5 * 128, 128)] = jnp.where(low, eb[:, pl.ds(QL + middle, 128)], om[l, :, pl.ds(middle, 128)])

    def att_partner(l):
        k2 = dfb_index(l)
        side, outer = side_of(l)
        partner = other[PAIR[l]]
        pairs[l].ready()
        pairs[k2].ready()
        len_cp[l].wait()
        c0 = here(az.at[l, partner], psend.at[0], stsem.at[0])
        c1 = here(az.at[k2, partner], psend.at[1], stsem.at[1])
        c0.wait()
        c1.wait()
        wab[...] = psend[0].astype(BF16)
        wdfb[...] = psend[1].astype(BF16)
        far = pl.ds(T, T)
        LT[0, :, far] = wab[...].T
        LT[1, :, far] = wdfb[...].T
        for k in range(3):
            wcols = jnp.concatenate([wq[l, k, :, pl.ds(outer, 128)], wq[l, k, :, pl.ds(middle, 128)]], axis=1)
            AB[0, 0, :, pl.ds(k * 256, 256)] = dot(wab[...], wcols).astype(BF16)
        wrows = jnp.concatenate([wo[l, pl.ds(outer, 128), :], wo[l, pl.ds(middle, 128), :]], axis=0)
        AB[0, 0, :, pl.ds(3 * 256, 256)] = dot_t(wdfb[...], wrows).astype(BF16)
        low = side == 0

        def window(w, _):
            rows = pl.ds(pl.multiple_of(w * 128, 128), 128)
            dest = pl.ds(pl.multiple_of(T + w * 128, 128), 128)
            live = lane.astype(F32) < lens[1 + l, pl.ds(w, 1), :]
            for p in range(2):
                qq, kk, vv, do = (AB[0, 0, rows, pl.ds(k * 256 + p * 128, 128)] for k in range(4))
                kk, vv = halves(kk), halves(vv)
                pair = (slope_outer(0, side), slope_outer(1, side)) if p == 0 else (slope(2), slope(3))
                prob, out = attend(qq, kk, vv, live, pair)
                dq, dk, dv = attend_bwd(qq, kk, vv, prob, do)
                if p == 0:
                    for k, v in enumerate((dq, dk, dv, out)):
                        LA[dest, pl.ds(k * 128, 128)] = v
                else:
                    LA[dest, pl.ds(4 * 128, 128)] = jnp.where(low, dq, dv)
                    LA[dest, pl.ds(5 * 128, 128)] = jnp.where(low, dk, out)
            return 0

        lax.fori_loop(0, W, window, 0)

    def place(at):
        return tuple(at[a] for a in AXES)

    def att_views(l, ch):
        at = {a: slice(None) for a in AXES}
        views = []
        for axis, land in zip(ATT[l][ch], (RA1, RA2, RA3)):
            send = GA.at[(l, ch) + place({**at, axis: other[axis]})]
            at[axis] = me[axis]
            views.append((send, GA.at[(l, ch) + place(at)], land.at[l, ch], axis))
        return views

    att_cp = {}

    def att_send(l, ch, step):
        send, _, land, axis = att_views(l, ch)[step]
        att_cp[l, ch, step] = remote(send, land, at_s.at[l, ch, step], at_r.at[l, ch, step], peer(axis))

    def att_grad(l, ch):
        for b in range(3):
            cols = pl.ds((3 * ch + b) * 128, 128)
            left = LT.at[0] if 3 * ch + b in (0, 1, 2, 4) else LT.at[1] if 3 * ch + b == 3 else LT.at[me[PAIR[l]]]
            GA[l, ch, :, :, :, :, b] = dot(left[...], LA[:, cols]).reshape(2, 2, 2, 2, R, 128)
        att_send(l, ch, 0)

    def att_recv(l, ch, step):
        _, stay, land, _ = att_views(l, ch)[step]
        att_cp[l, ch, step].wait_recv()
        stay[...] = stay[...] + land[...]
        if step < 2:
            att_send(l, ch, step + 1)
            return
        axis = PAIR[l]
        side, outer = side_of(l)
        outer_cols = pl.ds(outer, 128)
        if ch == 0:
            moves = ((pl.ds(0, 3), oatt.at[l, pl.ds(0, 3), :, outer_cols]),)
        else:
            mid = pl.ds(middle, 128)
            moves = (
                (0, oatt.at[l, 3, :, outer_cols]),
                (1, oatt.at[l, 2 * side, :, mid]),
                (2, oatt.at[l, 1 + 2 * side, :, mid]),
            )
        for i, (b, dst) in enumerate(moves):
            n = ch + i
            far = GA.at[(l, ch) + place({**me, axis: other[axis]}) + (b,)]
            att_cp[l, "out", n] = remote(far, dst, ato_s.at[l, n], ato_r.at[l, n], peer(axis))
            att_cp[l, "own", n] = here(GA.at[(l, ch) + place(me) + (b,)], dst, atl.at[l, n])

    def att_done(l):
        for ch in range(2):
            for step in range(3):
                att_cp[l, ch, step].wait_send()
        for n in range(4):
            att_cp[l, "out", n].wait()
            att_cp[l, "own", n].wait()

    def qcols_of(l):
        A, B = SHARE[l]
        return pl.ds(pl.multiple_of((2 * me[A] + me[B]) * FQ, 128), FQ)

    def ffn_hidden(l):
        k2 = dfb_index(l)
        qcols = qcols_of(l)

        def load(s):
            zz, xx = lax.div(s, 2), lax.rem(s, 2)
            return (
                pltpu.make_async_copy(ag.at[l, zz, xx], psend.at[0], stsem.at[0]),
                pltpu.make_async_copy(ag.at[k2, zz, xx], psend.at[1], stsem.at[1]),
            )

        for cp in load(0):
            cp.start()

        def chunk(s, _):
            zz, xx = lax.div(s, 2), lax.rem(s, 2)
            for cp in load(s):
                cp.wait()
            wab[...] = psend[0].astype(BF16)
            wdfb[...] = psend[1].astype(BF16)

            @pl.when(s < GROUP - 1)
            def _():
                for cp in load(s + 1):
                    cp.start()

            toks = pl.ds(pl.multiple_of(s * T, T), T)
            abT[:, toks] = wab[...].T
            dfbT[:, toks] = wdfb[...].T
            g = dot(wab[...], wi[l, 0, :, qcols])
            u = dot(wab[...], wi[l, 1, :, qcols])
            de = dot_t(wdfb[...], wd[l, qcols, :])
            act, slope_g = gelu_parts(g)
            AB[zz, xx, :, pl.ds(0, FQ)] = (de * u * slope_g).astype(BF16)
            AB[zz, xx, :, pl.ds(FQ, FQ)] = (de * act).astype(BF16)
            AB[zz, xx, :, pl.ds(2 * FQ, FQ)] = (act * u).astype(BF16)
            return 0

        lax.fori_loop(0, GROUP, chunk, 0)

    ffn_cp = {}
    kinds = (pl.ds(0, 2), pl.ds(2, 1))

    def sum_axes(l):
        return [a for a in AXES if a not in SHARE[l]]

    def ffn_block(l, i):
        (A, B), (r0, r1) = SHARE[l], sum_axes(l)
        to0, to1 = i in (0, 1), i in (0, 2)
        at0, at1 = other[r0] if to0 else me[r0], other[r1] if to1 else me[r1]
        base = at0 * weight[r0] + at1 * weight[r1]
        places = [base + i * weight[A] + j * weight[B] for i in range(2) for j in range(2)]
        for k in range(3):
            left = abT if k < 2 else dfbT
            rows = jnp.concatenate([left[pl.ds(pl.multiple_of(p * R, 16), R), :] for p in places], axis=0)
            right = jnp.concatenate([AB[i, j, :, pl.ds(k * FQ, FQ)] for i in range(2) for j in range(2)], axis=0)
            GF[l, at0, at1, k] = dot(rows, right)
        for ch in range(2):
            if i == 0:
                ffn_send(l, ch, 0)
            elif i == (1 if FFN[l][ch][0] == r0 else 2):
                ffn_send(l, ch, 1)

    def ffn_views(l, ch):
        k = kinds[ch]
        first, second = FFN[l][ch]

        def block(at):
            return GF.at[(l,) + tuple(at[a] for a in sum_axes(l)) + (k,)]

        both, one, two = {first: other[first], second: other[second]}, {**me, first: other[first]}, {**me, second: other[second]}
        return (
            (block(both), block(two), RF1.at[l, 0, k], first),
            (block(one), block(me), RF1.at[l, 1, k], first),
            (block(two), block(me), RF2.at[l, k], second),
        )

    def ffn_send(l, ch, i):
        src, _, land, axis = ffn_views(l, ch)[i]
        ffn_cp[l, ch, i] = remote(src, land, fz_s.at[l, ch, i], fz_r.at[l, ch, i], peer(axis))

    def ffn_recv(l, ch, i):
        _, stay, land, _ = ffn_views(l, ch)[i]
        ffn_cp[l, ch, i].wait_recv()
        stay[...] = stay[...] + land[...]
        if i == 0:
            ffn_send(l, ch, 2)
        if i < 2:
            return
        dst = offn.at[l, kinds[ch], :, qcols_of(l)]
        A, B = SHARE[l]
        final = [me[a] for a in sum_axes(l)]

        def rows_of(i, j):
            return GF.at[l, final[0], final[1], kinds[ch], pl.ds(pl.multiple_of((2 * i + j) * R, 16), R), :]

        ffn_cp[l, ch, "out"] = [
            remote(rows_of(i, j), dst, fa_s.at[l, ch, n], fa_r.at[l, ch, n], to)
            for n, (i, j, to) in enumerate(
                ((me[A], other[B], peer(B)), (other[A], me[B], peer(A)), (other[A], other[B], peer(A, B)))
            )
        ]
        ffn_cp[l, ch, "own"] = here(rows_of(me[A], me[B]), dst, fl.at[l, ch])

    def ffn_done(l):
        for ch in range(2):
            for i in range(3):
                ffn_cp[l, ch, i].wait_send()
            for cp in ffn_cp[l, ch, "out"]:
                cp.wait()
            ffn_cp[l, ch, "own"].wait()

    gn_cp = {}

    def gn_send(step):
        gn_cp[step] = remote(gn, gnr.at[step], gn_s.at[step], gn_r.at[step], peer(AXES[step]))

    def gn_recv(step):
        gn_cp[step].wait()
        gn[...] = gn[...] + gnr[step]
        if step < 3:
            gn_send(step + 1)

    x_cp.wait()
    for rows in row_chunks:
        xcur[rows, :] = ab[rows, :].astype(F32)
    cps = fwd_attention(0)
    fwd_norm1(0, cps)
    cps = fwd_ffn(0)
    fwd_norm2(0, cps)
    cps = fwd_attention(1, mid=pairs[0].share)
    fwd_norm1(1, cps)
    cps = fwd_ffn(1)
    cot_cp = here(cot_hbm, ab, insem.at[1])
    fwd_norm2(1, cps)

    cot_cp.wait()
    bwd_norm2(1, lambda rows: ab[rows, :].astype(F32))
    groups[0].forward()
    pairs[1].share()
    cps = bwd_ffn(1)
    bwd_norm1(1, cps)
    cps = bwd_attention(1, late=groups[1].forward)
    att_own(1)
    groups[0].share()
    bwd_input(1, cps)
    groups[2].forward()
    groups[2].sent()
    groups[2].own.wait()
    bwd_norm2(0, lambda rows: xcur[rows, :])
    cps = bwd_ffn(0)
    bwd_norm1(0, cps)
    pairs[2].share()
    gn_send(0)
    cps = bwd_attention(0, late=groups[1].share)
    bwd_input(0, cps)
    groups[2].share()
    igrad_cp = here(xcur, igrad_ref, igl.at[0])
    att_partner(1)
    groups[3].forward()
    att_grad(1, 0)
    att_grad(1, 1)
    gn_recv(0)
    groups[1].ready()
    groups[2].ready()
    ffn_hidden(1)
    for i in range(4):
        ffn_block(1, i)
    pairs[3].share()
    groups[3].share()
    gn_recv(1)
    att_own(0)
    att_partner(0)
    att_recv(1, 1, 0)
    att_grad(0, 0)
    att_grad(0, 1)
    gn_recv(2)
    groups[0].ready()
    groups[3].own.wait()
    groups[3].ready()
    ffn_hidden(0)
    att_recv(1, 0, 0)
    gn_recv(3)
    ffn_block(0, 0)
    ffn_recv(1, 1, 0)
    ffn_block(0, 1)
    ffn_block(0, 2)
    ffn_block(0, 3)
    ffn_recv(1, 1, 1)
    att_recv(1, 1, 1)
    ffn_recv(1, 0, 0)
    ffn_recv(0, 0, 0)
    ffn_recv(0, 0, 1)
    ffn_recv(1, 0, 1)
    ffn_recv(0, 1, 0)
    att_recv(1, 0, 1)
    ffn_recv(0, 1, 1)
    att_recv(1, 1, 2)
    att_recv(1, 0, 2)
    ffn_recv(1, 1, 2)
    att_recv(0, 0, 0)
    ffn_recv(0, 1, 2)
    att_recv(0, 1, 0)
    att_recv(0, 0, 1)
    att_recv(0, 1, 1)
    ffn_recv(0, 0, 2)
    ffn_recv(1, 0, 2)
    att_recv(0, 0, 2)
    att_recv(0, 1, 2)

    igrad_cp.wait()
    for k in (0, 1, 3):
        groups[k].sent()
    for l in range(L):
        att_done(l)
        ffn_done(l)


def fused(inputs, lengths, w_qkv, w_out, w_in, w_down, norm_gain, norm_bias, cotangent):
    T, D = inputs.shape
    L, _, _, E = w_qkv.shape
    F = w_in.shape[-1]
    W, NP, NC, FQ = T // 128, E // 128, D // 256, F // GROUP
    R = D // DP
    RB = 4 * R
    vmem = pl.BlockSpec(memory_space=pltpu.VMEM)
    smem = pl.BlockSpec(memory_space=pltpu.SMEM)
    hbm = pl.BlockSpec(memory_space=pl.ANY)
    V = pltpu.VMEM
    DMA = pltpu.SemaphoreType.DMA
    scratch = [
        V((L, 3, D, E), BF16), V((L, E, D), BF16), V((L, 2, D, F), BF16), V((L, F, D), BF16),
        V((L, T, D), BF16), V((L, 3, T, E), BF16), V((L, W, NP, 128, 256), BF16), V((L, T, E), BF16),
        V((L, T, D), BF16), V((L, T, D), BF16), V((L, T, 1), F32), V((L, T, 1), F32),
        V((T, D), F32), V((T, D), F32), V((T, D), BF16),
        V((2, T, D), F32), V((2, T, D), F32),
        V((T, F), BF16), V((L, 2, T, F), BF16),
        V((2, D, 2 * T), BF16), V((2 * T, 6 * 128), BF16),
        V((D, GROUP * T), BF16), V((D, GROUP * T), BF16),
        V((T, D), BF16), V((T, D), BF16), V((1 + L, 8, 128), F32),
        V((L, 2, 2, 3, RB, FQ), F32), V((L, 2, 3, RB, FQ), F32), V((L, 3, RB, FQ), F32),
        V((L, 2, 2, 2, 2, 2, 3, R, 128), F32),
        V((L, 2, 2, 2, 2, 3, R, 128), F32), V((L, 2, 2, 2, 3, R, 128), F32), V((L, 2, 2, 3, R, 128), F32),
        V((4, 4 * L, D), F32),
        DMA((L, 4)), DMA((2,)), DMA((2, NC)), DMA((2, NC)),
        DMA((2 * L,)), DMA((2 * L,)), DMA((2 * L,)), DMA((2 * L,)), DMA((2 * L,)), DMA((2 * L,)), DMA((2 * L,)),
        DMA((2 * L, 3)), DMA((2 * L, 3)),
        DMA((L,)), DMA((L,)), DMA((1,)),
        DMA((2 * L,)), DMA((2 * L,)), DMA((2 * L,)), DMA((2 * L,)), DMA((2 * L,)),
        DMA((2,)), DMA((L, 2, 3)), DMA((L, 2, 3)), DMA((L, 2, 3)), DMA((L, 2, 3)), DMA((L, 2)),
        DMA((L, 2, 3)), DMA((L, 2, 3)), DMA((L, 4)), DMA((L, 4)), DMA((L, 4)),
        DMA((4,)), DMA((4,)),
    ]
    outs = pl.pallas_call(
        functools.partial(kernel, T, D, E, F, L),
        out_shape=(
            jax.ShapeDtypeStruct((T, D), BF16),
            jax.ShapeDtypeStruct((T, D), F32),
            jax.ShapeDtypeStruct((L, 4, R, E), F32),
            jax.ShapeDtypeStruct((L, 3, R, F), F32),
            jax.ShapeDtypeStruct((4 * L, D), F32),
            jax.ShapeDtypeStruct((2 * L, 2, 2, T, D), F32),
            jax.ShapeDtypeStruct((2 * L, 2, T, D), F32),
        ),
        in_specs=[smem, hbm, hbm, vmem, vmem, hbm, hbm, hbm, hbm],
        out_specs=(vmem, hbm, hbm, hbm, vmem, hbm, hbm),
        scratch_shapes=scratch,
        compiler_params=pltpu.CompilerParams(collective_id=0, has_side_effects=True, vmem_limit_bytes=63 * 2**20),
        name="encoder",
    )(lengths, inputs, cotangent, norm_gain, norm_bias, w_qkv, w_out, w_in, w_down)
    encoded, input_grad, oatt, offn, gn, _, _ = outs
    mine = lax.dynamic_slice_in_dim(gn.reshape(2, L, 2, D), lax.axis_index("dp") * R, R, axis=3)
    return (
        encoded,
        input_grad,
        oatt[:, :3],
        jnp.swapaxes(oatt[:, 3], 1, 2),
        offn[:, :2],
        jnp.swapaxes(offn[:, 2], 1, 2),
        mine[0],
        mine[1],
    )


def normalize(values, gain_vec, shift_vec):
    center = values - jnp.mean(values, -1, keepdims=True)
    spread = jnp.mean(center * center, -1, keepdims=True)
    return center * lax.rsqrt(spread + EPS) * gain_vec + shift_vec


def gating(gate_pre, up_pre):
    return jax.nn.gelu(gate_pre, approximate=False) * up_pre


def head_bias(heads_local, length):
    first_head = lax.axis_index("tensor") * heads_local
    head_order = (first_head + jnp.arange(heads_local, dtype=jnp.int32)).astype(jnp.float32)
    slopes = 2.0 ** (-8.0 * (head_order + 1.0) / HEADS)
    places = jnp.arange(length, dtype=jnp.int32)
    distance = jnp.abs(places[:, None] - places[None, :]).astype(jnp.float32)
    return -slopes[:, None, None] * distance


def scores_of(query_heads, key_heads, bias_table, key_live):
    score_scale = query_heads.shape[-1] ** (-0.5)
    raw_scores = (
        jnp.einsum("wqhe,wkhe->whqk", query_heads, key_heads, preferred_element_type=jnp.float32)
        * score_scale
        + bias_table[None]
    )
    return jnp.where(key_live[:, None, None, :], raw_scores, MASKED)


def layer_forward(layer_rows, params, bias_table, key_live):
    qkv_weight, out_weight, in_weight, down_weight, gains_now, shifts_now = params
    windows, length = key_live.shape
    heads_local = bias_table.shape[0]
    rows_low = layer_rows.astype(jnp.bfloat16)
    projected = jnp.einsum(
        "td,cde->cte", rows_low, qkv_weight, preferred_element_type=jnp.float32
    ).astype(jnp.bfloat16)
    heads_split = projected.reshape(3, windows, length, heads_local, HEAD_DIM)
    scores = scores_of(heads_split[0], heads_split[1], bias_table, key_live)
    row_max = jnp.max(scores, -1, keepdims=True)
    log_total = row_max + jnp.log(jnp.sum(jnp.exp(scores - row_max), -1, keepdims=True))
    weights_low = jnp.exp(scores - log_total).astype(jnp.bfloat16)
    mixed_heads = jnp.einsum(
        "whqk,wkhe->wqhe", weights_low, heads_split[2], preferred_element_type=jnp.float32
    )
    mixed_heads = mixed_heads.astype(jnp.bfloat16).reshape(windows * length, heads_local * HEAD_DIM)
    attended = lax.psum(
        jnp.dot(mixed_heads, out_weight, preferred_element_type=jnp.float32), "tensor"
    )
    hidden = layer_rows + attended
    normed = normalize(hidden, gains_now[0], shifts_now[0])
    normed_low = normed.astype(jnp.bfloat16)
    gate_up = jnp.einsum("td,cdf->ctf", normed_low, in_weight, preferred_element_type=jnp.float32)
    gated_low = gating(gate_up[0], gate_up[1]).astype(jnp.bfloat16)
    fed_back = lax.psum(
        jnp.dot(gated_low, down_weight, preferred_element_type=jnp.float32), "tensor"
    )
    summed = normed + fed_back
    output = normalize(summed, gains_now[1], shifts_now[1])
    stored = (
        rows_low,
        projected,
        log_total,
        mixed_heads,
        hidden,
        normed_low,
        gate_up,
        gated_low,
        summed,
    )
    return (output, stored)


def layer_backward(grad_output, stored, params, bias_table, key_live):
    rows_low, projected, log_total, mixed_heads, hidden, normed_low, gate_up, gated_low, summed = (
        stored
    )
    qkv_weight, out_weight, in_weight, down_weight, gains_now, shifts_now = params
    windows, length = key_live.shape
    heads_local = bias_table.shape[0]
    _, pull_second = jax.vjp(normalize, summed, gains_now[1], shifts_now[1])
    grad_summed, gain_second, shift_second = pull_second(grad_output)
    grad_fed = grad_summed.astype(jnp.bfloat16)
    grad_gated = jnp.einsum("td,fd->tf", grad_fed, down_weight, preferred_element_type=jnp.float32)
    grad_down = jnp.einsum("tf,td->fd", gated_low, grad_fed, preferred_element_type=jnp.float32)
    _, pull_gate = jax.vjp(gating, gate_up[0], gate_up[1])
    grad_gate_pre, grad_up_pre = pull_gate(grad_gated)
    grad_gate_up = jnp.stack([grad_gate_pre, grad_up_pre]).astype(jnp.bfloat16)
    ffn_back = lax.psum(
        jnp.einsum("ctf,cdf->td", grad_gate_up, in_weight, preferred_element_type=jnp.float32),
        "tensor",
    )
    grad_in = jnp.einsum(
        "td,ctf->cdf", normed_low, grad_gate_up, preferred_element_type=jnp.float32
    )
    grad_normed = grad_summed + ffn_back
    _, pull_first = jax.vjp(normalize, hidden, gains_now[0], shifts_now[0])
    grad_hidden, gain_first, shift_first = pull_first(grad_normed)
    grad_attended = grad_hidden.astype(jnp.bfloat16)
    grad_mixed = jnp.einsum(
        "td,ed->te", grad_attended, out_weight, preferred_element_type=jnp.float32
    ).astype(jnp.bfloat16)
    grad_out_proj = jnp.einsum(
        "te,td->ed", mixed_heads, grad_attended, preferred_element_type=jnp.float32
    )
    heads_split = projected.reshape(3, windows, length, heads_local, HEAD_DIM)
    scores = scores_of(heads_split[0], heads_split[1], bias_table, key_live)
    probabilities = jnp.exp(scores - log_total)
    probs_low = probabilities.astype(jnp.bfloat16)
    grad_heads = grad_mixed.reshape(windows, length, heads_local, HEAD_DIM)
    grad_probs = jnp.einsum(
        "wqhe,wkhe->whqk", grad_heads, heads_split[2], preferred_element_type=jnp.float32
    )
    grad_values = jnp.einsum(
        "whqk,wqhe->wkhe", probs_low, grad_heads, preferred_element_type=jnp.float32
    )
    row_dot = jnp.sum(probabilities * grad_probs, -1, keepdims=True)
    grad_scores = (probabilities * (grad_probs - row_dot)).astype(jnp.bfloat16)
    score_scale = HEAD_DIM ** (-0.5)
    grad_query = (
        jnp.einsum(
            "whqk,wkhe->wqhe", grad_scores, heads_split[1], preferred_element_type=jnp.float32
        )
        * score_scale
    )
    grad_keys = (
        jnp.einsum(
            "whqk,wqhe->wkhe", grad_scores, heads_split[0], preferred_element_type=jnp.float32
        )
        * score_scale
    )
    grad_projected = jnp.stack([grad_query, grad_keys, grad_values]).astype(jnp.bfloat16)
    grad_projected = grad_projected.reshape(3, windows * length, heads_local * HEAD_DIM)
    attn_back = lax.psum(
        jnp.einsum("cte,cde->td", grad_projected, qkv_weight, preferred_element_type=jnp.float32),
        "tensor",
    )
    grad_qkv = jnp.einsum(
        "td,cte->cde", rows_low, grad_projected, preferred_element_type=jnp.float32
    )
    grad_rows = grad_hidden + attn_back
    grad_gains = jnp.stack([gain_first, gain_second])
    grad_shifts = jnp.stack([shift_first, shift_second])
    return (grad_rows, (grad_qkv, grad_out_proj, grad_in, grad_down, grad_gains, grad_shifts))


def body(inputs, lengths, w_qkv, w_out, w_in, w_down, norm_gain, norm_bias, cotangent):
    windows = lengths.shape[0]
    length = inputs.shape[0] // windows
    heads_local = w_qkv.shape[-1] // HEAD_DIM
    bias_table = head_bias(heads_local, length)
    key_live = jnp.arange(length, dtype=jnp.int32)[None, :] < lengths[:, None]
    layers = w_qkv.shape[0]
    layer_rows = inputs.astype(jnp.float32)
    stored_all = []
    for layer_index in range(layers):
        params = (
            w_qkv[layer_index],
            w_out[layer_index],
            w_in[layer_index],
            w_down[layer_index],
            norm_gain[layer_index],
            norm_bias[layer_index],
        )
        layer_rows, stored = layer_forward(layer_rows, params, bias_table, key_live)
        stored_all.append(stored)
    encoded = layer_rows.astype(jnp.bfloat16)
    grad_rows = cotangent.astype(jnp.float32)
    pieces = [None] * layers
    for layer_index in reversed(range(layers)):
        params = (
            w_qkv[layer_index],
            w_out[layer_index],
            w_in[layer_index],
            w_down[layer_index],
            norm_gain[layer_index],
            norm_bias[layer_index],
        )
        grad_rows, layer_grads = layer_backward(
            grad_rows, stored_all[layer_index], params, bias_table, key_live
        )
        pieces[layer_index] = layer_grads
    stacked = [jnp.stack([pieces[index][member] for index in range(layers)]) for member in range(6)]
    stacked = (
        lax.psum_scatter(stacked[0], "dp", scatter_dimension=2, tiled=True),
        lax.psum_scatter(stacked[1], "dp", scatter_dimension=2, tiled=True),
        lax.psum_scatter(stacked[2], "dp", scatter_dimension=2, tiled=True),
        lax.psum_scatter(stacked[3], "dp", scatter_dimension=2, tiled=True),
        lax.psum_scatter(stacked[4], "dp", scatter_dimension=2, tiled=True),
        lax.psum_scatter(stacked[5], "dp", scatter_dimension=2, tiled=True),
    )
    return (
        encoded,
        grad_rows,
        stacked[0],
        stacked[1],
        stacked[2],
        stacked[3],
        stacked[4],
        stacked[5],
    )


def solution(mesh):
    return jax.shard_map(
        fused if mesh.shape["dp"] == DP and mesh.shape["tensor"] == 2 else body,
        mesh=mesh,
        in_specs=(
            P("dp", None),
            P("dp"),
            P(None, None, None, "tensor"),
            P(None, "tensor", None),
            P(None, None, None, "tensor"),
            P(None, "tensor", None),
            P(),
            P(),
            P("dp", None),
        ),
        out_specs=(
            P("dp", None),
            P("dp", None),
            P(None, None, "dp", "tensor"),
            P(None, "tensor", "dp"),
            P(None, None, "dp", "tensor"),
            P(None, "tensor", "dp"),
            P(None, None, "dp"),
            P(None, None, "dp"),
        ),
        check_vma=False,
    )
```

```python
import functools

import jax
import jax.numpy as jnp
from jax import lax
from jax.experimental import pallas as pl
from jax.experimental.pallas import tpu as pltpu
from jax.sharding import PartitionSpec as P

HEADS = 12
HEAD_DIM = 64
EPS = 1e-05
MASKED = -1000000000.0
MESH = pl.DeviceIdType.MESH
F32 = jnp.float32
BF16 = jnp.bfloat16
GROUP = 4
DP = 16
AXES = ("z1", "z0", "y", "x")
SHARE = (("z1", "y"), ("z0", "x"))
FFN = ((("x", "z0"), ("z0", "x")), (("y", "z1"), ("z1", "y")))
PAIR = ("z0", "y")
ATT = ((("x", "y", "z1"), ("y", "x", "z1")), (("z0", "x", "z1"), ("x", "z0", "z1")))


def dot(a, b):
    return lax.dot_general(a, b, (((1,), (0,)), ((), ())), preferred_element_type=F32)


def dot_t(a, b):
    return lax.dot_general(a, b, (((1,), (1,)), ((), ())), preferred_element_type=F32)


def dot_tt(a, b):
    return lax.dot_general(a, b, (((0,), (0,)), ((), ())), preferred_element_type=F32)


def gelu_parts(g):
    bell = jnp.exp(-0.5 * g * g)
    d = 1.0 + (0.3275911 * 0.7071067811865476) * jnp.abs(g)
    t = pl.reciprocal(d, approx=True)
    t = t * (2.0 - d * t)
    poly = t * (0.127414796 + t * (-0.142248368 + t * (0.7107068705 + t * (-0.7265760135 + t * 0.5307027145))))
    tail = poly * bell
    phi = jnp.where(g >= 0, 1.0 - tail, tail)
    return g * phi, phi + g * (bell * 0.3989422804014327)


def kernel(
    T, D, E, F, L,
    len_ref, x_hbm, cot_hbm, gain_ref, bias_ref, wq_hbm, wo_hbm, wi_hbm, wd_hbm,
    enc_ref, igrad_ref, oatt, offn, gn, ag, az,
    wq, wo, wi, wd, xb, qkv, pb, om, hhat, zhat, hr, zr, xcur, acur, ab, psend, precv, eb, AB,
    LT, LA, abT, dfbT, stage, wab, wdfb, lens, GF, RF1, RF2, GA, RA1, RA2, RA3, gnr,
    wsem, insem, ps_s, ps_r, agl, aga_s, aga_r, agb_s, agb_r, agf_s, agf_r, agc_s, agc_r,
    ln_s, ln_r, igl, azl, azz_s, azz_r, azc_s, azc_r, stsem, fz_s, fz_r, fa_s, fa_r, fl, at_s, at_r, ato_s, ato_r, atl, gn_s, gn_r,
):
    dp = lax.axis_index("dp")
    c = lax.axis_index("tensor")
    weight = {"x": 1, "y": 2, "z0": 4, "z1": 8}
    me = {a: lax.rem(lax.div(dp, w), 2) for a, w in weight.items()}
    other = {a: 1 - me[a] for a in AXES}

    def peer(*axes):
        return (dp + sum(weight[a] * (1 - 2 * me[a]) for a in axes), c)

    sib = (dp, 1 - c)
    W = T // 128
    NP = E // 128
    FQ = F // GROUP
    NC = D // 256
    R = D // DP
    HT = T // 2
    QL = E

    def here(src, dst, sem):
        cp = pltpu.make_async_copy(src, dst, sem)
        cp.start()
        return cp

    wcopies = {}
    weights = ((wq_hbm, wq), (wo_hbm, wo), (wi_hbm, wi), (wd_hbm, wd))

    def load_weights(l):
        for i, (src, dst) in enumerate(weights):
            wcopies[l, i] = here(src.at[l], dst.at[l], wsem.at[l, i])

    x_cp = here(x_hbm, ab, insem.at[0])
    load_weights(0)

    barrier = pltpu.get_barrier_semaphore()
    friends = [sib] + [peer(a) for a in AXES] + [peer(*p) for p in sorted(set(SHARE))]
    for friend in friends:
        pl.semaphore_signal(barrier, inc=1, device_id=friend, device_id_type=MESH)
    pl.semaphore_wait(barrier, len(friends))

    def remote(src, dst, ss, rs, to):
        cp = pltpu.make_async_remote_copy(
            src_ref=src, dst_ref=dst, send_sem=ss, recv_sem=rs, device_id=to, device_id_type=MESH
        )
        cp.start()
        return cp

    RC = 64
    row_chunks = [pl.ds(r, RC) for r in range(0, T, RC)]

    def psum_send(slot, part):
        cps = []
        for n in range(NC):
            cols = pl.ds(n * 256, 256)
            psend[slot, :, cols] = part(n)
            cps.append(remote(psend.at[slot, :, cols], precv.at[slot, :, cols], ps_s.at[slot, n], ps_r.at[slot, n], sib))
        return cps

    def psum_wait(cps):
        for cp in cps:
            cp.wait()

    def psum_rows(slot, rows):
        return psend[slot, rows, :] + precv[slot, rows, :]

    def norm_rows(v):
        center = v - jnp.mean(v, -1, keepdims=True)
        r = lax.rsqrt(jnp.mean(center * center, -1, keepdims=True) + EPS)
        return center * r, r

    def ln_bwd_rows(dy, hat, r, gain):
        t = dy * gain
        m1 = jnp.mean(t, -1, keepdims=True)
        m2 = jnp.mean(t * hat, -1, keepdims=True)
        return r * (t - m1 - hat * m2)

    half = pl.ds(pl.multiple_of(c * HT, 128), HT)

    class Group:
        def __init__(self, k):
            A, B = SHARE[min(k, 2 * L - 1 - k)]
            self.k, self.A, self.B = k, A, B
            self.slots = {"own": (me[A], me[B]), "A": (other[A], me[B]), "B": (me[A], other[B]), "AB": (other[A], other[B])}

        def slot(self, name):
            i, j = self.slots[name]
            return ag.at[self.k, i, j]

        def keep(self, src):
            self.own = here(src, self.slot("own"), agl.at[self.k])

        def send(self, src=None):
            k = self.k
            mine = self.slot("own").at[half]
            if src is None:
                self.own.wait()
                src = mine
            else:
                src = src.at[half]
            self.ac = remote(src, mine, aga_s.at[k], aga_r.at[k], peer(self.A))
            self.bc = remote(src, mine, agb_s.at[k], agb_r.at[k], peer(self.B))

        def forward(self):
            k = self.k
            self.ac.wait_recv()
            ref = self.slot("A").at[half]
            self.fc = remote(ref, ref, agf_s.at[k], agf_r.at[k], peer(self.B))

        def share(self):
            k = self.k
            self.bc.wait_recv()
            self.fc.wait_recv()
            self.cc = []
            for j, name in enumerate(("A", "B", "AB")):
                ref = self.slot(name).at[half]
                self.cc.append(remote(ref, ref, agc_s.at[k, j], agc_r.at[k, j], sib))

        def sent(self):
            self.ac.wait_send()
            self.bc.wait_send()

        def ready(self):
            for cp in self.cc:
                cp.wait()
            self.fc.wait_send()

    class Pair:
        def __init__(self, k):
            self.k, self.axis = k, PAIR[min(k, 2 * L - 1 - k)]

        def keep(self, src):
            self.own = here(src, az.at[self.k, me[self.axis]], azl.at[self.k])

        def send(self):
            k = self.k
            self.own.wait()
            mine = az.at[k, me[self.axis], half]
            self.zc = remote(mine, mine, azz_s.at[k], azz_r.at[k], peer(self.axis))

        def share(self):
            k = self.k
            self.zc.wait()
            ref = az.at[k, other[self.axis], half]
            self.cc = remote(ref, ref, azc_s.at[k], azc_r.at[k], sib)

        def ready(self):
            self.cc.wait()

    for w in range(W):
        lens[0, pl.ds(w, 1), :] = jnp.full((1, 128), len_ref[w], jnp.int32).astype(F32)
    len_cp = [remote(lens.at[0], lens.at[1 + l], ln_s.at[l], ln_r.at[l], peer(PAIR[l])) for l in range(L)]

    def dfb_index(l):
        return 2 * L - 1 - l

    groups = [Group(k) for k in range(2 * L)]
    pairs = [Pair(k) for k in range(2 * L)]

    lane = lax.broadcasted_iota(jnp.int32, (128, 128), 1)
    first = lane < HEAD_DIM
    dist = jnp.abs(lax.broadcasted_iota(jnp.int32, (128, 128), 0) - lane).astype(F32)
    scale = HEAD_DIM ** -0.5

    def halves(v):
        zero = jnp.zeros_like(v)
        return jnp.concatenate([jnp.where(first, v, zero), jnp.where(first, zero, v)], axis=0)

    def pick(table, index):
        s = jnp.float32(table[0])
        for i in range(1, len(table)):
            s = jnp.where(index == i, jnp.float32(table[i]), s)
        return s

    heads_local = E // HEAD_DIM
    slopes = [2.0 ** (-8.0 * (h + 1.0) / HEADS) for h in range(HEADS)]

    def slope(h):
        return pick(slopes[h::heads_local], c)

    def slope_outer(i, side):
        table = []
        for cc in range(HEADS // heads_local):
            table += [slopes[cc * heads_local + i], slopes[cc * heads_local + 2 * (NP - 1) + i]]
        return pick(table, 2 * c + side)

    def attend(qq, kk, vv, live, slope_pair):
        s = dot_t(qq, kk)
        both = []
        for i in range(2):
            si = s[:, i * 128:(i + 1) * 128] * scale - slope_pair[i] * dist
            si = jnp.where(live, si, MASKED)
            ei = jnp.exp(si - jnp.max(si, -1, keepdims=True))
            both.append(ei * (1.0 / jnp.sum(ei, -1, keepdims=True)))
        prob = jnp.concatenate(both, axis=1).astype(BF16)
        return prob, dot(prob, vv).astype(BF16)

    def attend_bwd(qq, kk, vv, prob, do):
        dprob = dot_t(do, vv)
        p32 = prob.astype(F32)
        both = []
        for i in range(2):
            pi, di = p32[:, i * 128:(i + 1) * 128], dprob[:, i * 128:(i + 1) * 128]
            both.append(pi * (di - jnp.sum(pi * di, -1, keepdims=True)))
        ds = jnp.concatenate(both, axis=1).astype(BF16)
        dv2 = dot_tt(prob, do)
        dk2 = dot_tt(ds, qq)
        dq = (dot(ds, kk) * scale).astype(BF16)
        dk = (jnp.where(first, dk2[:128], dk2[128:]) * scale).astype(BF16)
        dv = jnp.where(first, dv2[:128], dv2[128:]).astype(BF16)
        return dq, dk, dv

    sums = {}

    def proj(l):
        pairs[l].keep(xcur)
        for rows in row_chunks:
            xb[l, rows, :] = xcur[rows, :].astype(BF16)
        wcopies[l, 0].wait()
        if l == 0:
            for later in range(1, L):
                load_weights(later)
        out = dot(xb[l], jnp.concatenate([wq[l, k] for k in range(3)], axis=1)).astype(BF16)
        for k in range(3):
            qkv[l, k] = out[:, k * E:(k + 1) * E]
        pairs[l].send()

    def win(l):
        for w in range(W):
            rows = pl.ds(w * 128, 128)
            live = lane < len_ref[w]
            for p in range(NP):
                cols = pl.ds(p * 128, 128)
                kk, vv = halves(qkv[l, 1, rows, cols]), halves(qkv[l, 2, rows, cols])
                prob, out = attend(qkv[l, 0, rows, cols], kk, vv, live, (slope(2 * p), slope(2 * p + 1)))
                pb[l, w, p] = prob
                om[l, rows, cols] = out

    def out_sum(l):
        wcopies[l, 1].wait()
        sums[0] = psum_send(0, lambda n: dot(om[l], wo[l, :, pl.ds(n * 256, 256)]))

    def norm1(l):
        psum_wait(sums[0])
        gain, bias = gain_ref[l, 0:1, :], bias_ref[l, 0:1, :]
        for rows in row_chunks:
            hat, r = norm_rows(xcur[rows, :] + psum_rows(0, rows))
            hhat[l, rows, :] = hat.astype(BF16)
            hr[l, rows, :] = r
            a = hat * gain + bias
            acur[rows, :] = a
            ab[rows, :] = a.astype(BF16)
        groups[l].keep(acur)

    def hidden(l, chunks):
        if chunks[0] == 0:
            wcopies[l, 2].wait()
        for j in chunks:
            cols = pl.ds(j * 256, 256)
            g = dot(ab[...], wi[l, 0, :, cols])
            u = dot(ab[...], wi[l, 1, :, cols])
            act, slope_g = gelu_parts(g)
            eb[:, cols] = (act * u).astype(BF16)
            AB[l, 0, :, cols] = act.astype(BF16)
            AB[l, 1, :, cols] = (slope_g * u).astype(BF16)

    def down_sum(l):
        wcopies[l, 3].wait()
        sums[1] = psum_send(1, lambda n: dot(eb[...], wd[l, :, pl.ds(n * 256, 256)]))

    def norm2(l):
        psum_wait(sums[1])
        gain, bias = gain_ref[l, 1:2, :], bias_ref[l, 1:2, :]
        for rows in row_chunks:
            hat, r = norm_rows(acur[rows, :] + psum_rows(1, rows))
            zhat[l, rows, :] = hat.astype(BF16)
            zr[l, rows, :] = r
            out = hat * gain + bias
            if l == L - 1:
                enc_ref[rows, :] = out.astype(BF16)
            else:
                xcur[rows, :] = out

    def bwd_norm2(l, dy_rows):
        gain = gain_ref[l, 1:2, :]
        dg = jnp.zeros((1, D), F32)
        db = jnp.zeros((1, D), F32)
        for rows in row_chunks:
            dy = dy_rows(rows)
            hat = zhat[l, rows, :].astype(F32)
            dz = ln_bwd_rows(dy, hat, zr[l, rows, :], gain)
            acur[rows, :] = dz
            ab[rows, :] = dz.astype(BF16)
            dg = dg + jnp.sum(dy * hat, 0, keepdims=True)
            db = db + jnp.sum(dy, 0, keepdims=True)
        gn[pl.ds(2 * l + 1, 1), :] = dg
        gn[pl.ds(2 * L + 2 * l + 1, 1), :] = db
        if l == 0:
            groups[dfb_index(l)].send(acur)
        groups[dfb_index(l)].keep(acur)

    def bwd_hidden(l):
        for j in range(F // 256):
            cols = pl.ds(j * 256, 256)
            de = dot_t(ab[...], wd[l, cols, :])
            dg = de * AB[l, 1, :, cols].astype(F32)
            du = de * AB[l, 0, :, cols].astype(F32)
            AB[l, 0, :, cols] = dg.astype(BF16)
            AB[l, 1, :, cols] = du.astype(BF16)
        if l > 0:
            groups[dfb_index(l)].send()

    def hidden_sum(l):
        def part(n):
            rows = pl.ds(n * 256, 256)
            return dot_t(AB[l, 0], wi[l, 0, rows, :]) + dot_t(AB[l, 1], wi[l, 1, rows, :])

        sums[0] = psum_send(0, part)

    def bwd_norm1(l):
        psum_wait(sums[0])
        gain = gain_ref[l, 0:1, :]
        dg = jnp.zeros((1, D), F32)
        db = jnp.zeros((1, D), F32)
        for rows in row_chunks:
            da = acur[rows, :] + psum_rows(0, rows)
            hat = hhat[l, rows, :].astype(F32)
            dh = ln_bwd_rows(da, hat, hr[l, rows, :], gain)
            xcur[rows, :] = dh
            ab[rows, :] = dh.astype(BF16)
            dg = dg + jnp.sum(da * hat, 0, keepdims=True)
            db = db + jnp.sum(da, 0, keepdims=True)
        gn[pl.ds(2 * l, 1), :] = dg
        gn[pl.ds(2 * L + 2 * l, 1), :] = db
        pairs[dfb_index(l)].keep(xcur)

    def dqkv(k):
        return pl.ds(k * QL, QL)

    def dob(l):
        eb[:, dqkv(3)] = dot_t(ab[...], wo[l]).astype(BF16)
        pairs[dfb_index(l)].send()

    def bwd_win(l):
        for w in range(W):
            rows = pl.ds(w * 128, 128)
            for p in range(NP):
                cols = pl.ds(p * 128, 128)
                kk, vv = halves(qkv[l, 1, rows, cols]), halves(qkv[l, 2, rows, cols])
                grads = attend_bwd(qkv[l, 0, rows, cols], kk, vv, pb[l, w, p], eb[rows, pl.ds(3 * QL + p * 128, 128)])
                for k in range(3):
                    eb[rows, pl.ds(k * QL + p * 128, 128)] = grads[k]

    def qkv_sum(l):
        def part(n):
            rows = pl.ds(n * 256, 256)
            return dot_t(eb[:, pl.ds(0, 3 * QL)], jnp.concatenate([wq[l, k, rows, :] for k in range(3)], axis=1))

        sums[1] = psum_send(1, part)

    def bwd_input(l):
        psum_wait(sums[1])
        for rows in row_chunks:
            dx = xcur[rows, :] + psum_rows(1, rows)
            xcur[rows, :] = dx

    middle = 128

    def side_of(l):
        side = me[PAIR[l]]
        return side, pl.multiple_of(side * (E - 128), 128)

    def att_own(l):
        side, outer = side_of(l)
        own = pl.ds(0, T)
        LT[0, :, own] = xb[l].T
        LT[1, :, own] = ab[...].T
        for k in range(3):
            LA[own, pl.ds(k * 128, 128)] = eb[:, pl.ds(pl.multiple_of(k * QL + outer, 128), 128)]
        LA[own, pl.ds(3 * 128, 128)] = om[l, :, pl.ds(outer, 128)]
        low = side == 0
        LA[own, pl.ds(4 * 128, 128)] = jnp.where(low, eb[:, pl.ds(middle, 128)], eb[:, pl.ds(2 * QL + middle, 128)])
        LA[own, pl.ds(5 * 128, 128)] = jnp.where(low, eb[:, pl.ds(QL + middle, 128)], om[l, :, pl.ds(middle, 128)])

    att_loads = {}

    def att_load(l):
        k2, partner = dfb_index(l), other[PAIR[l]]
        pairs[l].ready()
        pairs[k2].ready()
        att_loads[l] = here(az.at[l, partner], stage.at[0], stsem.at[0, 0]), here(az.at[k2, partner], stage.at[1], stsem.at[0, 1])

    def att_partner(l):
        side, outer = side_of(l)
        len_cp[l].wait()
        c0, c1 = att_loads.pop(l)
        c0.wait()
        c1.wait()
        wab[...] = stage[0].astype(BF16)
        wdfb[...] = stage[1].astype(BF16)
        far = pl.ds(T, T)
        LT[0, :, far] = wab[...].T
        LT[1, :, far] = wdfb[...].T
        wcols = jnp.concatenate([wq[l, k, :, pl.ds(at, 128)] for k in range(3) for at in (outer, middle)], axis=1)
        AB[0, 0, :, pl.ds(0, 3 * 256)] = dot(wab[...], wcols).astype(BF16)
        wrows = jnp.concatenate([wo[l, pl.ds(outer, 128), :], wo[l, pl.ds(middle, 128), :]], axis=0)
        AB[0, 0, :, pl.ds(3 * 256, 256)] = dot_t(wdfb[...], wrows).astype(BF16)
        low = side == 0

        for w in range(W):
            rows = pl.ds(w * 128, 128)
            dest = pl.ds(T + w * 128, 128)
            live = lane.astype(F32) < lens[1 + l, pl.ds(w, 1), :]
            for p in range(2):
                qq, kk, vv, do = (AB[0, 0, rows, pl.ds(k * 256 + p * 128, 128)] for k in range(4))
                kk, vv = halves(kk), halves(vv)
                pair = (slope_outer(0, side), slope_outer(1, side)) if p == 0 else (slope(2), slope(3))
                prob, out = attend(qq, kk, vv, live, pair)
                dq, dk, dv = attend_bwd(qq, kk, vv, prob, do)
                if p == 0:
                    for k, v in enumerate((dq, dk, dv, out)):
                        LA[dest, pl.ds(k * 128, 128)] = v
                else:
                    LA[dest, pl.ds(4 * 128, 128)] = jnp.where(low, dq, dv)
                    LA[dest, pl.ds(5 * 128, 128)] = jnp.where(low, dk, out)

    def place(at):
        return tuple(at[a] for a in AXES)

    def att_views(l, ch):
        at = {a: slice(None) for a in AXES}
        views = []
        for axis, land in zip(ATT[l][ch], (RA1, RA2, RA3)):
            send = GA.at[(l, ch) + place({**at, axis: other[axis]})]
            at[axis] = me[axis]
            views.append((send, GA.at[(l, ch) + place(at)], land.at[l, ch], axis))
        return views

    att_cp = {}

    def att_send(l, ch, step):
        send, _, land, axis = att_views(l, ch)[step]
        att_cp[l, ch, step] = remote(send, land, at_s.at[l, ch, step], at_r.at[l, ch, step], peer(axis))

    def att_grad(l, ch):
        for b in range(3):
            cols = pl.ds((3 * ch + b) * 128, 128)
            left = LT.at[0] if 3 * ch + b in (0, 1, 2, 4) else LT.at[1] if 3 * ch + b == 3 else LT.at[me[PAIR[l]]]
            GA[l, ch, :, :, :, :, b] = dot(left[...], LA[:, cols]).reshape(2, 2, 2, 2, R, 128)
        att_send(l, ch, 0)

    def att_recv(l, ch, step):
        _, stay, land, _ = att_views(l, ch)[step]
        att_cp[l, ch, step].wait_recv()
        stay[...] = stay[...] + land[...]
        if step < 2:
            att_send(l, ch, step + 1)
            return
        axis = PAIR[l]
        side, outer = side_of(l)
        outer_cols = pl.ds(outer, 128)
        if ch == 0:
            moves = ((pl.ds(0, 3), oatt.at[l, pl.ds(0, 3), :, outer_cols]),)
        else:
            mid = pl.ds(middle, 128)
            moves = (
                (0, oatt.at[l, 3, :, outer_cols]),
                (1, oatt.at[l, 2 * side, :, mid]),
                (2, oatt.at[l, 1 + 2 * side, :, mid]),
            )
        for i, (b, dst) in enumerate(moves):
            n = ch + i
            far = GA.at[(l, ch) + place({**me, axis: other[axis]}) + (b,)]
            att_cp[l, "out", n] = remote(far, dst, ato_s.at[l, n], ato_r.at[l, n], peer(axis))
            att_cp[l, "own", n] = here(GA.at[(l, ch) + place(me) + (b,)], dst, atl.at[l, n])

    def att_done(l):
        for ch in range(2):
            for step in range(3):
                att_cp[l, ch, step].wait_send()
        for n in range(4):
            att_cp[l, "out", n].wait()
            att_cp[l, "own", n].wait()

    def qcols_of(l):
        A, B = SHARE[l]
        return pl.ds(pl.multiple_of((2 * me[A] + me[B]) * FQ, 128), FQ)

    ffn_loads = {}

    def ffn_load_one(l, s):
        i, j = s // 2, s % 2
        buf = (psend, precv)[s % 2]
        return [here(ag.at[k, i, j], buf.at[n], stsem.at[1 + s % 2, n]) for n, k in enumerate((l, dfb_index(l)))]

    def ffn_load(l):
        groups[l].ready()
        groups[dfb_index(l)].ready()
        ffn_loads[l] = [ffn_load_one(l, 0), ffn_load_one(l, 1)]

    def ffn_hidden(l):
        qcols = qcols_of(l)

        loads = ffn_loads.pop(l)
        for s in range(GROUP):
            buf = (psend, precv)[s % 2]
            for cp in loads[s]:
                cp.wait()
            wab[...] = buf[0].astype(BF16)
            wdfb[...] = buf[1].astype(BF16)
            if s + 2 < GROUP:
                loads.append(ffn_load_one(l, s + 2))
            toks = pl.ds(s * T, T)
            abT[:, toks] = wab[...].T
            dfbT[:, toks] = wdfb[...].T
            gu = dot(wab[...], jnp.concatenate([wi[l, 0, :, qcols], wi[l, 1, :, qcols]], axis=1))
            de = dot_t(wdfb[...], wd[l, qcols, :])
            g, u = gu[:, :FQ], gu[:, FQ:]
            act, slope_g = gelu_parts(g)
            AB[s // 2, s % 2, :, pl.ds(0, FQ)] = (de * u * slope_g).astype(BF16)
            AB[s // 2, s % 2, :, pl.ds(FQ, FQ)] = (de * act).astype(BF16)
            AB[s // 2, s % 2, :, pl.ds(2 * FQ, FQ)] = (act * u).astype(BF16)

    ffn_cp = {}
    kinds = (pl.ds(0, 2), pl.ds(2, 1))

    def sum_axes(l):
        return [a for a in AXES if a not in SHARE[l]]

    def ffn_block(l, i):
        (A, B), (r0, r1) = SHARE[l], sum_axes(l)
        to0, to1 = i in (0, 1), i in (0, 2)
        at0, at1 = other[r0] if to0 else me[r0], other[r1] if to1 else me[r1]
        base = at0 * weight[r0] + at1 * weight[r1]
        places = [base + i * weight[A] + j * weight[B] for i in range(2) for j in range(2)]
        for left, k, n in ((abT, 0, 2), (dfbT, 2, 1)):
            rows = jnp.concatenate([left[pl.ds(pl.multiple_of(p * R, 16), R), :] for p in places], axis=0)
            right = jnp.concatenate([AB[i, j, :, pl.ds(k * FQ, n * FQ)] for i in range(2) for j in range(2)], axis=0)
            out = dot(rows, right)
            for m in range(n):
                GF[l, at0, at1, k + m] = out[:, m * FQ:(m + 1) * FQ]
        for ch in range(2):
            if i == 0:
                ffn_send(l, ch, 0)
            elif i == (1 if FFN[l][ch][0] == r0 else 2):
                ffn_send(l, ch, 1)

    def ffn_views(l, ch):
        k = kinds[ch]
        first, second = FFN[l][ch]

        def block(at):
            return GF.at[(l,) + tuple(at[a] for a in sum_axes(l)) + (k,)]

        both, one, two = {first: other[first], second: other[second]}, {**me, first: other[first]}, {**me, second: other[second]}
        return (
            (block(both), block(two), RF1.at[l, 0, k], first),
            (block(one), block(me), RF1.at[l, 1, k], first),
            (block(two), block(me), RF2.at[l, k], second),
        )

    def ffn_send(l, ch, i):
        src, _, land, axis = ffn_views(l, ch)[i]
        ffn_cp[l, ch, i] = remote(src, land, fz_s.at[l, ch, i], fz_r.at[l, ch, i], peer(axis))

    def ffn_recv(l, ch, i):
        _, stay, land, _ = ffn_views(l, ch)[i]
        ffn_cp[l, ch, i].wait_recv()
        stay[...] = stay[...] + land[...]
        if i == 0:
            ffn_send(l, ch, 2)
        if i < 2:
            return
        dst = offn.at[l, kinds[ch], :, qcols_of(l)]
        A, B = SHARE[l]
        final = [me[a] for a in sum_axes(l)]

        def rows_of(i, j):
            return GF.at[l, final[0], final[1], kinds[ch], pl.ds(pl.multiple_of((2 * i + j) * R, 16), R), :]

        ffn_cp[l, ch, "out"] = [
            remote(rows_of(i, j), dst, fa_s.at[l, ch, n], fa_r.at[l, ch, n], to)
            for n, (i, j, to) in enumerate(
                ((me[A], other[B], peer(B)), (other[A], me[B], peer(A)), (other[A], other[B], peer(A, B)))
            )
        ]
        ffn_cp[l, ch, "own"] = here(rows_of(me[A], me[B]), dst, fl.at[l, ch])

    def ffn_done(l):
        for ch in range(2):
            for i in range(3):
                ffn_cp[l, ch, i].wait_send()
            for cp in ffn_cp[l, ch, "out"]:
                cp.wait()
            ffn_cp[l, ch, "own"].wait()

    gn_cp = {}

    def gn_send(step):
        gn_cp[step] = remote(gn, gnr.at[step], gn_s.at[step], gn_r.at[step], peer(AXES[step]))

    def gn_recv(step):
        gn_cp[step].wait()
        gn[...] = gn[...] + gnr[step]
        if step < 3:
            gn_send(step + 1)

    x_cp.wait()
    for rows in row_chunks:
        xcur[rows, :] = ab[rows, :].astype(F32)
    proj(0)
    win(0)
    out_sum(0)
    norm1(0)
    hidden(0, range(2))
    groups[0].send()
    hidden(0, range(2, F // 256))
    down_sum(0)
    norm2(0)
    proj(1)
    win(1)
    out_sum(1)
    norm1(1)
    hidden(1, range(2))
    groups[1].send()
    hidden(1, range(2, F // 256))
    cot_cp = here(cot_hbm, ab, insem.at[1])
    down_sum(1)
    pairs[0].share()
    norm2(1)
    cot_cp.wait()
    bwd_norm2(1, lambda rows: ab[rows, :].astype(F32))
    bwd_hidden(1)
    hidden_sum(1)
    pairs[1].share()
    bwd_norm1(1)
    groups[0].forward()
    dob(1)
    bwd_win(1)
    qkv_sum(1)
    att_own(1)
    groups[1].forward()
    bwd_input(1)
    bwd_norm2(0, lambda rows: xcur[rows, :])
    bwd_hidden(0)
    hidden_sum(0)
    groups[0].share()
    bwd_norm1(0)
    gn_send(0)
    dob(0)
    bwd_win(0)
    qkv_sum(0)
    bwd_input(0)
    igrad_cp = here(xcur, igrad_ref, igl.at[0])
    groups[1].share()
    groups[2].forward()
    pairs[2].share()
    att_load(1)
    att_partner(1)
    gn_recv(0)
    att_grad(1, 0)
    att_grad(1, 1)
    groups[3].forward()
    groups[2].share()
    pairs[3].share()
    ffn_load(1)
    ffn_hidden(1)
    gn_recv(1)
    groups[3].share()
    for i in range(4):
        ffn_block(1, i)
    att_load(0)
    att_own(0)
    att_partner(0)
    gn_recv(2)
    att_recv(1, 1, 0)
    att_grad(0, 0)
    att_grad(0, 1)
    groups[3].own.wait()
    ffn_load(0)
    ffn_hidden(0)
    gn_recv(3)
    att_recv(1, 0, 0)
    for i in range(4):
        ffn_block(0, i)
    ffn_recv(1, 0, 0)
    ffn_recv(1, 1, 0)
    att_recv(0, 0, 0)
    att_recv(1, 1, 1)
    att_recv(1, 0, 1)
    ffn_recv(1, 0, 1)
    ffn_recv(1, 1, 1)
    ffn_recv(0, 1, 0)
    ffn_recv(0, 0, 0)
    att_recv(0, 1, 0)
    ffn_recv(1, 1, 2)
    ffn_recv(0, 1, 1)
    att_recv(0, 0, 1)
    ffn_recv(0, 0, 1)
    ffn_recv(1, 0, 2)
    ffn_recv(0, 1, 2)
    att_recv(1, 1, 2)
    att_recv(0, 1, 1)
    att_recv(1, 0, 2)
    ffn_recv(0, 0, 2)
    att_recv(0, 0, 2)
    att_recv(0, 1, 2)

    igrad_cp.wait()
    for k in range(2 * L):
        groups[k].sent()
    for l in range(L):
        att_done(l)
        ffn_done(l)


def fused(inputs, lengths, w_qkv, w_out, w_in, w_down, norm_gain, norm_bias, cotangent):
    T, D = inputs.shape
    L, _, _, E = w_qkv.shape
    F = w_in.shape[-1]
    W, NP, NC, FQ = T // 128, E // 128, D // 256, F // GROUP
    R = D // DP
    RB = 4 * R
    vmem = pl.BlockSpec(memory_space=pltpu.VMEM)
    smem = pl.BlockSpec(memory_space=pltpu.SMEM)
    hbm = pl.BlockSpec(memory_space=pl.ANY)
    V = pltpu.VMEM
    DMA = pltpu.SemaphoreType.DMA
    scratch = [
        V((L, 3, D, E), BF16), V((L, E, D), BF16), V((L, 2, D, F), BF16), V((L, F, D), BF16),
        V((L, T, D), BF16), V((L, 3, T, E), BF16), V((L, W, NP, 128, 256), BF16), V((L, T, E), BF16),
        V((L, T, D), BF16), V((L, T, D), BF16), V((L, T, 1), F32), V((L, T, 1), F32),
        V((T, D), F32), V((T, D), F32), V((T, D), BF16),
        V((2, T, D), F32), V((2, T, D), F32),
        V((T, F), BF16), V((L, 2, T, F), BF16),
        V((2, D, 2 * T), BF16), V((2 * T, 6 * 128), BF16),
        V((D, GROUP * T), BF16), V((D, GROUP * T), BF16),
        V((2, T, D), F32), V((T, D), BF16), V((T, D), BF16), V((1 + L, 8, 128), F32),
        V((L, 2, 2, 3, RB, FQ), F32), V((L, 2, 3, RB, FQ), F32), V((L, 3, RB, FQ), F32),
        V((L, 2, 2, 2, 2, 2, 3, R, 128), F32),
        V((L, 2, 2, 2, 2, 3, R, 128), F32), V((L, 2, 2, 2, 3, R, 128), F32), V((L, 2, 2, 3, R, 128), F32),
        V((4, 4 * L, D), F32),
        DMA((L, 4)), DMA((2,)), DMA((2, NC)), DMA((2, NC)),
        DMA((2 * L,)), DMA((2 * L,)), DMA((2 * L,)), DMA((2 * L,)), DMA((2 * L,)), DMA((2 * L,)), DMA((2 * L,)),
        DMA((2 * L, 3)), DMA((2 * L, 3)),
        DMA((L,)), DMA((L,)), DMA((1,)),
        DMA((2 * L,)), DMA((2 * L,)), DMA((2 * L,)), DMA((2 * L,)), DMA((2 * L,)),
        DMA((3, 2)), DMA((L, 2, 3)), DMA((L, 2, 3)), DMA((L, 2, 3)), DMA((L, 2, 3)), DMA((L, 2)),
        DMA((L, 2, 3)), DMA((L, 2, 3)), DMA((L, 4)), DMA((L, 4)), DMA((L, 4)),
        DMA((4,)), DMA((4,)),
    ]
    outs = pl.pallas_call(
        functools.partial(kernel, T, D, E, F, L),
        out_shape=(
            jax.ShapeDtypeStruct((T, D), BF16),
            jax.ShapeDtypeStruct((T, D), F32),
            jax.ShapeDtypeStruct((L, 4, R, E), F32),
            jax.ShapeDtypeStruct((L, 3, R, F), F32),
            jax.ShapeDtypeStruct((4 * L, D), F32),
            jax.ShapeDtypeStruct((2 * L, 2, 2, T, D), F32),
            jax.ShapeDtypeStruct((2 * L, 2, T, D), F32),
        ),
        in_specs=[smem, hbm, hbm, vmem, vmem, hbm, hbm, hbm, hbm],
        out_specs=(vmem, hbm, hbm, hbm, vmem, hbm, hbm),
        scratch_shapes=scratch,
        compiler_params=pltpu.CompilerParams(collective_id=0, has_side_effects=True, vmem_limit_bytes=63 * 2**20),
        name="encoder",
    )(lengths, inputs, cotangent, norm_gain, norm_bias, w_qkv, w_out, w_in, w_down)
    encoded, input_grad, oatt, offn, gn, _, _ = outs
    mine = lax.dynamic_slice_in_dim(gn.reshape(2, L, 2, D), lax.axis_index("dp") * R, R, axis=3)
    return (
        encoded,
        input_grad,
        oatt[:, :3],
        jnp.swapaxes(oatt[:, 3], 1, 2),
        offn[:, :2],
        jnp.swapaxes(offn[:, 2], 1, 2),
        mine[0],
        mine[1],
    )


def normalize(values, gain_vec, shift_vec):
    center = values - jnp.mean(values, -1, keepdims=True)
    spread = jnp.mean(center * center, -1, keepdims=True)
    return center * lax.rsqrt(spread + EPS) * gain_vec + shift_vec


def gating(gate_pre, up_pre):
    return jax.nn.gelu(gate_pre, approximate=False) * up_pre


def head_bias(heads_local, length):
    first_head = lax.axis_index("tensor") * heads_local
    head_order = (first_head + jnp.arange(heads_local, dtype=jnp.int32)).astype(jnp.float32)
    slopes = 2.0 ** (-8.0 * (head_order + 1.0) / HEADS)
    places = jnp.arange(length, dtype=jnp.int32)
    distance = jnp.abs(places[:, None] - places[None, :]).astype(jnp.float32)
    return -slopes[:, None, None] * distance


def scores_of(query_heads, key_heads, bias_table, key_live):
    score_scale = query_heads.shape[-1] ** (-0.5)
    raw_scores = (
        jnp.einsum("wqhe,wkhe->whqk", query_heads, key_heads, preferred_element_type=jnp.float32)
        * score_scale
        + bias_table[None]
    )
    return jnp.where(key_live[:, None, None, :], raw_scores, MASKED)


def layer_forward(layer_rows, params, bias_table, key_live):
    qkv_weight, out_weight, in_weight, down_weight, gains_now, shifts_now = params
    windows, length = key_live.shape
    heads_local = bias_table.shape[0]
    rows_low = layer_rows.astype(jnp.bfloat16)
    projected = jnp.einsum(
        "td,cde->cte", rows_low, qkv_weight, preferred_element_type=jnp.float32
    ).astype(jnp.bfloat16)
    heads_split = projected.reshape(3, windows, length, heads_local, HEAD_DIM)
    scores = scores_of(heads_split[0], heads_split[1], bias_table, key_live)
    row_max = jnp.max(scores, -1, keepdims=True)
    log_total = row_max + jnp.log(jnp.sum(jnp.exp(scores - row_max), -1, keepdims=True))
    weights_low = jnp.exp(scores - log_total).astype(jnp.bfloat16)
    mixed_heads = jnp.einsum(
        "whqk,wkhe->wqhe", weights_low, heads_split[2], preferred_element_type=jnp.float32
    )
    mixed_heads = mixed_heads.astype(jnp.bfloat16).reshape(windows * length, heads_local * HEAD_DIM)
    attended = lax.psum(
        jnp.dot(mixed_heads, out_weight, preferred_element_type=jnp.float32), "tensor"
    )
    hidden = layer_rows + attended
    normed = normalize(hidden, gains_now[0], shifts_now[0])
    normed_low = normed.astype(jnp.bfloat16)
    gate_up = jnp.einsum("td,cdf->ctf", normed_low, in_weight, preferred_element_type=jnp.float32)
    gated_low = gating(gate_up[0], gate_up[1]).astype(jnp.bfloat16)
    fed_back = lax.psum(
        jnp.dot(gated_low, down_weight, preferred_element_type=jnp.float32), "tensor"
    )
    summed = normed + fed_back
    output = normalize(summed, gains_now[1], shifts_now[1])
    stored = (
        rows_low,
        projected,
        log_total,
        mixed_heads,
        hidden,
        normed_low,
        gate_up,
        gated_low,
        summed,
    )
    return (output, stored)


def layer_backward(grad_output, stored, params, bias_table, key_live):
    rows_low, projected, log_total, mixed_heads, hidden, normed_low, gate_up, gated_low, summed = (
        stored
    )
    qkv_weight, out_weight, in_weight, down_weight, gains_now, shifts_now = params
    windows, length = key_live.shape
    heads_local = bias_table.shape[0]
    _, pull_second = jax.vjp(normalize, summed, gains_now[1], shifts_now[1])
    grad_summed, gain_second, shift_second = pull_second(grad_output)
    grad_fed = grad_summed.astype(jnp.bfloat16)
    grad_gated = jnp.einsum("td,fd->tf", grad_fed, down_weight, preferred_element_type=jnp.float32)
    grad_down = jnp.einsum("tf,td->fd", gated_low, grad_fed, preferred_element_type=jnp.float32)
    _, pull_gate = jax.vjp(gating, gate_up[0], gate_up[1])
    grad_gate_pre, grad_up_pre = pull_gate(grad_gated)
    grad_gate_up = jnp.stack([grad_gate_pre, grad_up_pre]).astype(jnp.bfloat16)
    ffn_back = lax.psum(
        jnp.einsum("ctf,cdf->td", grad_gate_up, in_weight, preferred_element_type=jnp.float32),
        "tensor",
    )
    grad_in = jnp.einsum(
        "td,ctf->cdf", normed_low, grad_gate_up, preferred_element_type=jnp.float32
    )
    grad_normed = grad_summed + ffn_back
    _, pull_first = jax.vjp(normalize, hidden, gains_now[0], shifts_now[0])
    grad_hidden, gain_first, shift_first = pull_first(grad_normed)
    grad_attended = grad_hidden.astype(jnp.bfloat16)
    grad_mixed = jnp.einsum(
        "td,ed->te", grad_attended, out_weight, preferred_element_type=jnp.float32
    ).astype(jnp.bfloat16)
    grad_out_proj = jnp.einsum(
        "te,td->ed", mixed_heads, grad_attended, preferred_element_type=jnp.float32
    )
    heads_split = projected.reshape(3, windows, length, heads_local, HEAD_DIM)
    scores = scores_of(heads_split[0], heads_split[1], bias_table, key_live)
    probabilities = jnp.exp(scores - log_total)
    probs_low = probabilities.astype(jnp.bfloat16)
    grad_heads = grad_mixed.reshape(windows, length, heads_local, HEAD_DIM)
    grad_probs = jnp.einsum(
        "wqhe,wkhe->whqk", grad_heads, heads_split[2], preferred_element_type=jnp.float32
    )
    grad_values = jnp.einsum(
        "whqk,wqhe->wkhe", probs_low, grad_heads, preferred_element_type=jnp.float32
    )
    row_dot = jnp.sum(probabilities * grad_probs, -1, keepdims=True)
    grad_scores = (probabilities * (grad_probs - row_dot)).astype(jnp.bfloat16)
    score_scale = HEAD_DIM ** (-0.5)
    grad_query = (
        jnp.einsum(
            "whqk,wkhe->wqhe", grad_scores, heads_split[1], preferred_element_type=jnp.float32
        )
        * score_scale
    )
    grad_keys = (
        jnp.einsum(
            "whqk,wqhe->wkhe", grad_scores, heads_split[0], preferred_element_type=jnp.float32
        )
        * score_scale
    )
    grad_projected = jnp.stack([grad_query, grad_keys, grad_values]).astype(jnp.bfloat16)
    grad_projected = grad_projected.reshape(3, windows * length, heads_local * HEAD_DIM)
    attn_back = lax.psum(
        jnp.einsum("cte,cde->td", grad_projected, qkv_weight, preferred_element_type=jnp.float32),
        "tensor",
    )
    grad_qkv = jnp.einsum(
        "td,cte->cde", rows_low, grad_projected, preferred_element_type=jnp.float32
    )
    grad_rows = grad_hidden + attn_back
    grad_gains = jnp.stack([gain_first, gain_second])
    grad_shifts = jnp.stack([shift_first, shift_second])
    return (grad_rows, (grad_qkv, grad_out_proj, grad_in, grad_down, grad_gains, grad_shifts))


def body(inputs, lengths, w_qkv, w_out, w_in, w_down, norm_gain, norm_bias, cotangent):
    windows = lengths.shape[0]
    length = inputs.shape[0] // windows
    heads_local = w_qkv.shape[-1] // HEAD_DIM
    bias_table = head_bias(heads_local, length)
    key_live = jnp.arange(length, dtype=jnp.int32)[None, :] < lengths[:, None]
    layers = w_qkv.shape[0]
    layer_rows = inputs.astype(jnp.float32)
    stored_all = []
    for layer_index in range(layers):
        params = (
            w_qkv[layer_index],
            w_out[layer_index],
            w_in[layer_index],
            w_down[layer_index],
            norm_gain[layer_index],
            norm_bias[layer_index],
        )
        layer_rows, stored = layer_forward(layer_rows, params, bias_table, key_live)
        stored_all.append(stored)
    encoded = layer_rows.astype(jnp.bfloat16)
    grad_rows = cotangent.astype(jnp.float32)
    pieces = [None] * layers
    for layer_index in reversed(range(layers)):
        params = (
            w_qkv[layer_index],
            w_out[layer_index],
            w_in[layer_index],
            w_down[layer_index],
            norm_gain[layer_index],
            norm_bias[layer_index],
        )
        grad_rows, layer_grads = layer_backward(
            grad_rows, stored_all[layer_index], params, bias_table, key_live
        )
        pieces[layer_index] = layer_grads
    stacked = [jnp.stack([pieces[index][member] for index in range(layers)]) for member in range(6)]
    stacked = (
        lax.psum_scatter(stacked[0], "dp", scatter_dimension=2, tiled=True),
        lax.psum_scatter(stacked[1], "dp", scatter_dimension=2, tiled=True),
        lax.psum_scatter(stacked[2], "dp", scatter_dimension=2, tiled=True),
        lax.psum_scatter(stacked[3], "dp", scatter_dimension=2, tiled=True),
        lax.psum_scatter(stacked[4], "dp", scatter_dimension=2, tiled=True),
        lax.psum_scatter(stacked[5], "dp", scatter_dimension=2, tiled=True),
    )
    return (
        encoded,
        grad_rows,
        stacked[0],
        stacked[1],
        stacked[2],
        stacked[3],
        stacked[4],
        stacked[5],
    )


def solution(mesh):
    return jax.shard_map(
        fused if mesh.shape["dp"] == DP and mesh.shape["tensor"] == 2 else body,
        mesh=mesh,
        in_specs=(
            P("dp", None),
            P("dp"),
            P(None, None, None, "tensor"),
            P(None, "tensor", None),
            P(None, None, None, "tensor"),
            P(None, "tensor", None),
            P(),
            P(),
            P("dp", None),
        ),
        out_specs=(
            P("dp", None),
            P("dp", None),
            P(None, None, "dp", "tensor"),
            P(None, "tensor", "dp"),
            P(None, None, "dp", "tensor"),
            P(None, "tensor", "dp"),
            P(None, None, "dp"),
            P(None, None, "dp"),
        ),
        check_vma=False,
    )
```

```python
import functools

import jax
import jax.numpy as jnp
from jax import lax
from jax.experimental import pallas as pl
from jax.experimental.pallas import tpu as pltpu
from jax.sharding import PartitionSpec as P

HEADS = 12
HEAD_DIM = 64
EPS = 1e-05
MASKED = -1000000000.0
MESH = pl.DeviceIdType.MESH
F32 = jnp.float32
BF16 = jnp.bfloat16
GROUP = 4
DP = 16
AXES = ("z1", "z0", "y", "x")
SHARE = (("z1", "y"), ("z0", "x"))
FFN = ((("x", "z0"), ("z0", "x")), (("y", "z1"), ("z1", "y")))
PAIR = ("z0", "y")
ATT = ((("x", "y", "z1"), ("y", "x", "z1")), (("z0", "x", "z1"), ("x", "z0", "z1")))


def dot(a, b):
    return lax.dot_general(a, b, (((1,), (0,)), ((), ())), preferred_element_type=F32)


def dot_t(a, b):
    return lax.dot_general(a, b, (((1,), (1,)), ((), ())), preferred_element_type=F32)


def dot_tt(a, b):
    return lax.dot_general(a, b, (((0,), (0,)), ((), ())), preferred_element_type=F32)


def gelu_parts(g):
    bell = jnp.exp(-0.5 * g * g)
    d = 1.0 + (0.3275911 * 0.7071067811865476) * jnp.abs(g)
    t = pl.reciprocal(d, approx=True)
    t = t * (2.0 - d * t)
    poly = t * (0.127414796 + t * (-0.142248368 + t * (0.7107068705 + t * (-0.7265760135 + t * 0.5307027145))))
    tail = poly * bell
    phi = jnp.where(g >= 0, 1.0 - tail, tail)
    return g * phi, phi + g * (bell * 0.3989422804014327)


def kernel(
    T, D, E, F, L,
    len_ref, x_hbm, cot_hbm, gain_ref, bias_ref, wq_hbm, wo_hbm, wi_hbm, wd_hbm,
    enc_ref, igrad_ref, oatt, offn, gn, ag, az,
    wq, wo, wi, wd, xb, qkv, pb, om, hhat, zhat, hr, zr, xcur, acur, ab, psend, precv, eb, AB,
    LT, LA, abT, dfbT, stage, wab, wdfb, lens, GF, RF1, RF2, GA, RA1, RA2, RA3, gnr,
    wsem, insem, ps_s, ps_r, agl, aga_s, aga_r, agb_s, agb_r, agf_s, agf_r, agc_s, agc_r,
    ln_s, ln_r, igl, azl, azz_s, azz_r, azc_s, azc_r, stsem, fz_s, fz_r, fa_s, fa_r, fl, at_s, at_r, ato_s, ato_r, atl, gn_s, gn_r,
):
    dp = lax.axis_index("dp")
    c = lax.axis_index("tensor")
    weight = {"x": 1, "y": 2, "z0": 4, "z1": 8}
    me = {a: lax.rem(lax.div(dp, w), 2) for a, w in weight.items()}
    other = {a: 1 - me[a] for a in AXES}

    def peer(*axes):
        return (dp + sum(weight[a] * (1 - 2 * me[a]) for a in axes), c)

    sib = (dp, 1 - c)
    W = T // 128
    NP = E // 128
    FQ = F // GROUP
    NC = D // 256
    R = D // DP
    HT = T // 2
    QL = E

    def here(src, dst, sem):
        cp = pltpu.make_async_copy(src, dst, sem)
        cp.start()
        return cp

    wcopies = {}
    weights = ((wq_hbm, wq), (wo_hbm, wo), (wi_hbm, wi), (wd_hbm, wd))

    def load_weights(l):
        for i, (src, dst) in enumerate(weights):
            wcopies[l, i] = here(src.at[l], dst.at[l], wsem.at[l, i])

    x_cp = here(x_hbm, ab, insem.at[0])
    load_weights(0)

    barrier = pltpu.get_barrier_semaphore()
    friends = [sib] + [peer(a) for a in AXES] + [peer(*p) for p in sorted(set(SHARE))]
    for friend in friends:
        pl.semaphore_signal(barrier, inc=1, device_id=friend, device_id_type=MESH)
    pl.semaphore_wait(barrier, len(friends))

    def remote(src, dst, ss, rs, to):
        cp = pltpu.make_async_remote_copy(
            src_ref=src, dst_ref=dst, send_sem=ss, recv_sem=rs, device_id=to, device_id_type=MESH
        )
        cp.start()
        return cp

    RC = 64
    row_chunks = [pl.ds(r, RC) for r in range(0, T, RC)]

    def psum_send(slot, part):
        cps = []
        for n in range(NC):
            cols = pl.ds(n * 256, 256)
            psend[slot, :, cols] = part(n)
            cps.append(remote(psend.at[slot, :, cols], precv.at[slot, :, cols], ps_s.at[slot, n], ps_r.at[slot, n], sib))
        return cps

    def psum_wait(cps):
        for cp in cps:
            cp.wait()

    def psum_rows(slot, rows):
        return psend[slot, rows, :] + precv[slot, rows, :]

    def norm_rows(v):
        center = v - jnp.mean(v, -1, keepdims=True)
        r = lax.rsqrt(jnp.mean(center * center, -1, keepdims=True) + EPS)
        return center * r, r

    def ln_bwd_rows(dy, hat, r, gain):
        t = dy * gain
        m1 = jnp.mean(t, -1, keepdims=True)
        m2 = jnp.mean(t * hat, -1, keepdims=True)
        return r * (t - m1 - hat * m2)

    half = pl.ds(pl.multiple_of(c * HT, 128), HT)

    class Group:
        def __init__(self, k):
            A, B = SHARE[min(k, 2 * L - 1 - k)]
            self.k, self.A, self.B = k, A, B
            self.slots = {"own": (me[A], me[B]), "A": (other[A], me[B]), "B": (me[A], other[B]), "AB": (other[A], other[B])}

        def slot(self, name):
            i, j = self.slots[name]
            return ag.at[self.k, i, j]

        def keep(self, src):
            self.own = here(src, self.slot("own"), agl.at[self.k])

        def send(self, src=None):
            k = self.k
            mine = self.slot("own").at[half]
            if src is None:
                self.own.wait()
                src = mine
            else:
                src = src.at[half]
            self.ac = remote(src, mine, aga_s.at[k], aga_r.at[k], peer(self.A))
            self.bc = remote(src, mine, agb_s.at[k], agb_r.at[k], peer(self.B))

        def forward(self):
            k = self.k
            self.ac.wait_recv()
            ref = self.slot("A").at[half]
            self.fc = remote(ref, ref, agf_s.at[k], agf_r.at[k], peer(self.B))

        def share(self):
            k = self.k
            self.bc.wait_recv()
            self.fc.wait_recv()
            self.cc = []
            for j, name in enumerate(("A", "B", "AB")):
                ref = self.slot(name).at[half]
                self.cc.append(remote(ref, ref, agc_s.at[k, j], agc_r.at[k, j], sib))

        def sent(self):
            self.ac.wait_send()
            self.bc.wait_send()

        def ready(self):
            for cp in self.cc:
                cp.wait()
            self.fc.wait_send()

    class Pair:
        def __init__(self, k):
            self.k, self.axis = k, PAIR[min(k, 2 * L - 1 - k)]

        def keep(self, src):
            self.own = here(src, az.at[self.k, me[self.axis]], azl.at[self.k])

        def send(self):
            k = self.k
            self.own.wait()
            mine = az.at[k, me[self.axis], half]
            self.zc = remote(mine, mine, azz_s.at[k], azz_r.at[k], peer(self.axis))

        def share(self):
            k = self.k
            self.zc.wait()
            ref = az.at[k, other[self.axis], half]
            self.cc = remote(ref, ref, azc_s.at[k], azc_r.at[k], sib)

        def ready(self):
            self.cc.wait()

    for w in range(W):
        lens[0, pl.ds(w, 1), :] = jnp.full((1, 128), len_ref[w], jnp.int32).astype(F32)
    len_cp = [remote(lens.at[0], lens.at[1 + l], ln_s.at[l], ln_r.at[l], peer(PAIR[l])) for l in range(L)]

    def dfb_index(l):
        return 2 * L - 1 - l

    groups = [Group(k) for k in range(2 * L)]
    pairs = [Pair(k) for k in range(2 * L)]

    lane = lax.broadcasted_iota(jnp.int32, (128, 128), 1)
    first = lane < HEAD_DIM
    dist = jnp.abs(lax.broadcasted_iota(jnp.int32, (128, 128), 0) - lane).astype(F32)
    scale = HEAD_DIM ** -0.5

    def halves(v):
        zero = jnp.zeros_like(v)
        return jnp.concatenate([jnp.where(first, v, zero), jnp.where(first, zero, v)], axis=0)

    def pick(table, index):
        s = jnp.float32(table[0])
        for i in range(1, len(table)):
            s = jnp.where(index == i, jnp.float32(table[i]), s)
        return s

    heads_local = E // HEAD_DIM
    slopes = [2.0 ** (-8.0 * (h + 1.0) / HEADS) for h in range(HEADS)]

    def slope(h):
        return pick(slopes[h::heads_local], c)

    def slope_outer(i, side):
        table = []
        for cc in range(HEADS // heads_local):
            table += [slopes[cc * heads_local + i], slopes[cc * heads_local + 2 * (NP - 1) + i]]
        return pick(table, 2 * c + side)

    def attend(qq, kk, vv, live, slope_pair):
        s = dot_t(qq, kk)
        both = []
        for i in range(2):
            si = s[:, i * 128:(i + 1) * 128] * scale - slope_pair[i] * dist
            si = jnp.where(live, si, MASKED)
            ei = jnp.exp(si - jnp.max(si, -1, keepdims=True))
            both.append(ei * (1.0 / jnp.sum(ei, -1, keepdims=True)))
        prob = jnp.concatenate(both, axis=1).astype(BF16)
        return prob, dot(prob, vv).astype(BF16)

    def attend_bwd(qq, kk, vv, prob, do):
        dprob = dot_t(do, vv)
        p32 = prob.astype(F32)
        both = []
        for i in range(2):
            pi, di = p32[:, i * 128:(i + 1) * 128], dprob[:, i * 128:(i + 1) * 128]
            both.append(pi * (di - jnp.sum(pi * di, -1, keepdims=True)))
        ds = jnp.concatenate(both, axis=1).astype(BF16)
        dv2 = dot_tt(prob, do)
        dk2 = dot_tt(ds, qq)
        dq = (dot(ds, kk) * scale).astype(BF16)
        dk = (jnp.where(first, dk2[:128], dk2[128:]) * scale).astype(BF16)
        dv = jnp.where(first, dv2[:128], dv2[128:]).astype(BF16)
        return dq, dk, dv

    sums = {}

    def proj(l):
        pairs[l].keep(xcur)
        for rows in row_chunks:
            xb[l, rows, :] = xcur[rows, :].astype(BF16)
        wcopies[l, 0].wait()
        if l == 0:
            for later in range(1, L):
                load_weights(later)
        out = dot(xb[l], jnp.concatenate([wq[l, k] for k in range(3)], axis=1)).astype(BF16)
        for k in range(3):
            qkv[l, k] = out[:, k * E:(k + 1) * E]
        pairs[l].send()

    def win(l):
        for w in range(W):
            rows = pl.ds(w * 128, 128)
            live = lane < len_ref[w]
            for p in range(NP):
                cols = pl.ds(p * 128, 128)
                kk, vv = halves(qkv[l, 1, rows, cols]), halves(qkv[l, 2, rows, cols])
                prob, out = attend(qkv[l, 0, rows, cols], kk, vv, live, (slope(2 * p), slope(2 * p + 1)))
                pb[l, w, p] = prob
                om[l, rows, cols] = out

    def out_sum(l):
        wcopies[l, 1].wait()
        sums[0] = psum_send(0, lambda n: dot(om[l], wo[l, :, pl.ds(n * 256, 256)]))

    def norm1(l):
        psum_wait(sums[0])
        gain, bias = gain_ref[l, 0:1, :], bias_ref[l, 0:1, :]
        for rows in row_chunks:
            hat, r = norm_rows(xcur[rows, :] + psum_rows(0, rows))
            hhat[l, rows, :] = hat.astype(BF16)
            hr[l, rows, :] = r
            a = hat * gain + bias
            acur[rows, :] = a
            ab[rows, :] = a.astype(BF16)
        groups[l].keep(acur)

    def hidden(l, chunks):
        if chunks[0] == 0:
            wcopies[l, 2].wait()
        for j in chunks:
            cols = pl.ds(j * 256, 256)
            g = dot(ab[...], wi[l, 0, :, cols])
            u = dot(ab[...], wi[l, 1, :, cols])
            act, slope_g = gelu_parts(g)
            eb[:, cols] = (act * u).astype(BF16)
            AB[l, 0, :, cols] = act.astype(BF16)
            AB[l, 1, :, cols] = (slope_g * u).astype(BF16)

    def down_sum(l):
        wcopies[l, 3].wait()
        sums[1] = psum_send(1, lambda n: dot(eb[...], wd[l, :, pl.ds(n * 256, 256)]))

    def norm2(l):
        psum_wait(sums[1])
        gain, bias = gain_ref[l, 1:2, :], bias_ref[l, 1:2, :]
        for rows in row_chunks:
            hat, r = norm_rows(acur[rows, :] + psum_rows(1, rows))
            zhat[l, rows, :] = hat.astype(BF16)
            zr[l, rows, :] = r
            out = hat * gain + bias
            if l == L - 1:
                wab[rows, :] = out.astype(BF16)
            else:
                xcur[rows, :] = out
        if l == L - 1:
            sums["encoded"] = here(wab, enc_ref, insem.at[2])

    def bwd_norm2(l, dy_rows):
        gain = gain_ref[l, 1:2, :]
        dg = jnp.zeros((1, D), F32)
        db = jnp.zeros((1, D), F32)
        for rows in row_chunks:
            dy = dy_rows(rows)
            hat = zhat[l, rows, :].astype(F32)
            dz = ln_bwd_rows(dy, hat, zr[l, rows, :], gain)
            acur[rows, :] = dz
            ab[rows, :] = dz.astype(BF16)
            dg = dg + jnp.sum(dy * hat, 0, keepdims=True)
            db = db + jnp.sum(dy, 0, keepdims=True)
        gn[pl.ds(2 * l + 1, 1), :] = dg
        gn[pl.ds(2 * L + 2 * l + 1, 1), :] = db
        if l == 0:
            groups[dfb_index(l)].send(acur)
        groups[dfb_index(l)].keep(acur)

    def bwd_hidden(l):
        for j in range(F // 256):
            cols = pl.ds(j * 256, 256)
            de = dot_t(ab[...], wd[l, cols, :])
            dg = de * AB[l, 1, :, cols].astype(F32)
            du = de * AB[l, 0, :, cols].astype(F32)
            AB[l, 0, :, cols] = dg.astype(BF16)
            AB[l, 1, :, cols] = du.astype(BF16)
        if l > 0:
            groups[dfb_index(l)].send()

    def hidden_sum(l):
        def part(n):
            rows = pl.ds(n * 256, 256)
            return dot_t(AB[l, 0], wi[l, 0, rows, :]) + dot_t(AB[l, 1], wi[l, 1, rows, :])

        sums[0] = psum_send(0, part)

    def bwd_norm1(l):
        psum_wait(sums[0])
        if l == L - 1:
            sums["encoded"].wait()
        gain = gain_ref[l, 0:1, :]
        dg = jnp.zeros((1, D), F32)
        db = jnp.zeros((1, D), F32)
        for rows in row_chunks:
            da = acur[rows, :] + psum_rows(0, rows)
            hat = hhat[l, rows, :].astype(F32)
            dh = ln_bwd_rows(da, hat, hr[l, rows, :], gain)
            xcur[rows, :] = dh
            ab[rows, :] = dh.astype(BF16)
            dg = dg + jnp.sum(da * hat, 0, keepdims=True)
            db = db + jnp.sum(da, 0, keepdims=True)
        gn[pl.ds(2 * l, 1), :] = dg
        gn[pl.ds(2 * L + 2 * l, 1), :] = db
        pairs[dfb_index(l)].keep(xcur)

    def dqkv(k):
        return pl.ds(k * QL, QL)

    def dob(l):
        eb[:, dqkv(3)] = dot_t(ab[...], wo[l]).astype(BF16)
        pairs[dfb_index(l)].send()

    def bwd_win(l):
        def window(w, _):
            rows = pl.ds(pl.multiple_of(w * 128, 128), 128)
            for p in range(NP):
                cols = pl.ds(p * 128, 128)
                kk, vv = halves(qkv[l, 1, rows, cols]), halves(qkv[l, 2, rows, cols])
                grads = attend_bwd(qkv[l, 0, rows, cols], kk, vv, pb[l, w, p], eb[rows, pl.ds(3 * QL + p * 128, 128)])
                for k in range(3):
                    eb[rows, pl.ds(k * QL + p * 128, 128)] = grads[k]
            return 0

        lax.fori_loop(0, W, window, 0)

    def qkv_sum(l):
        def part(n):
            rows = pl.ds(n * 256, 256)
            return dot_t(eb[:, pl.ds(0, 3 * QL)], jnp.concatenate([wq[l, k, rows, :] for k in range(3)], axis=1))

        sums[1] = psum_send(1, part)

    def bwd_input(l):
        psum_wait(sums[1])
        for rows in row_chunks:
            dx = xcur[rows, :] + psum_rows(1, rows)
            xcur[rows, :] = dx

    middle = 128

    def side_of(l):
        side = me[PAIR[l]]
        return side, pl.multiple_of(side * (E - 128), 128)

    def att_own(l):
        side, outer = side_of(l)
        own = pl.ds(0, T)
        LT[0, :, own] = xb[l].T
        LT[1, :, own] = ab[...].T
        for k in range(3):
            LA[own, pl.ds(k * 128, 128)] = eb[:, pl.ds(pl.multiple_of(k * QL + outer, 128), 128)]
        LA[own, pl.ds(3 * 128, 128)] = om[l, :, pl.ds(outer, 128)]
        low = side == 0
        LA[own, pl.ds(4 * 128, 128)] = jnp.where(low, eb[:, pl.ds(middle, 128)], eb[:, pl.ds(2 * QL + middle, 128)])
        LA[own, pl.ds(5 * 128, 128)] = jnp.where(low, eb[:, pl.ds(QL + middle, 128)], om[l, :, pl.ds(middle, 128)])

    att_loads = {}

    def att_load(l):
        k2, partner = dfb_index(l), other[PAIR[l]]
        pairs[l].ready()
        pairs[k2].ready()
        att_loads[l] = here(az.at[l, partner], stage.at[0], stsem.at[0, 0]), here(az.at[k2, partner], stage.at[1], stsem.at[0, 1])

    def att_partner(l):
        side, outer = side_of(l)
        len_cp[l].wait()
        c0, c1 = att_loads.pop(l)
        c0.wait()
        c1.wait()
        wab[...] = stage[0].astype(BF16)
        wdfb[...] = stage[1].astype(BF16)
        far = pl.ds(T, T)
        LT[0, :, far] = wab[...].T
        LT[1, :, far] = wdfb[...].T
        wcols = jnp.concatenate([wq[l, k, :, pl.ds(at, 128)] for k in range(3) for at in (outer, middle)], axis=1)
        AB[0, 0, :, pl.ds(0, 3 * 256)] = dot(wab[...], wcols).astype(BF16)
        wrows = jnp.concatenate([wo[l, pl.ds(outer, 128), :], wo[l, pl.ds(middle, 128), :]], axis=0)
        AB[0, 0, :, pl.ds(3 * 256, 256)] = dot_t(wdfb[...], wrows).astype(BF16)
        low = side == 0

        def window(w, _):
            rows = pl.ds(pl.multiple_of(w * 128, 128), 128)
            dest = pl.ds(pl.multiple_of(T + w * 128, 128), 128)
            live = lane.astype(F32) < lens[1 + l, pl.ds(w, 1), :]
            for p in range(2):
                qq, kk, vv, do = (AB[0, 0, rows, pl.ds(k * 256 + p * 128, 128)] for k in range(4))
                kk, vv = halves(kk), halves(vv)
                pair = (slope_outer(0, side), slope_outer(1, side)) if p == 0 else (slope(2), slope(3))
                prob, out = attend(qq, kk, vv, live, pair)
                dq, dk, dv = attend_bwd(qq, kk, vv, prob, do)
                if p == 0:
                    for k, v in enumerate((dq, dk, dv, out)):
                        LA[dest, pl.ds(k * 128, 128)] = v
                else:
                    LA[dest, pl.ds(4 * 128, 128)] = jnp.where(low, dq, dv)
                    LA[dest, pl.ds(5 * 128, 128)] = jnp.where(low, dk, out)
            return 0

        lax.fori_loop(0, W, window, 0)

    def place(at):
        return tuple(at[a] for a in AXES)

    def att_views(l, ch):
        at = {a: slice(None) for a in AXES}
        views = []
        for axis, land in zip(ATT[l][ch], (RA1, RA2, RA3)):
            send = GA.at[(l, ch) + place({**at, axis: other[axis]})]
            at[axis] = me[axis]
            views.append((send, GA.at[(l, ch) + place(at)], land.at[l, ch], axis))
        return views

    att_cp = {}

    def att_send(l, ch, step):
        send, _, land, axis = att_views(l, ch)[step]
        att_cp[l, ch, step] = remote(send, land, at_s.at[l, ch, step], at_r.at[l, ch, step], peer(axis))

    def att_grad(l, ch):
        for b in range(3):
            cols = pl.ds((3 * ch + b) * 128, 128)
            left = LT.at[0] if 3 * ch + b in (0, 1, 2, 4) else LT.at[1] if 3 * ch + b == 3 else LT.at[me[PAIR[l]]]
            GA[l, ch, :, :, :, :, b] = dot(left[...], LA[:, cols]).reshape(2, 2, 2, 2, R, 128)
        att_send(l, ch, 0)

    def att_recv(l, ch, step):
        _, stay, land, _ = att_views(l, ch)[step]
        att_cp[l, ch, step].wait_recv()
        stay[...] = stay[...] + land[...]
        if step < 2:
            att_send(l, ch, step + 1)
            return
        axis = PAIR[l]
        side, outer = side_of(l)
        outer_cols = pl.ds(outer, 128)
        if ch == 0:
            moves = ((pl.ds(0, 3), oatt.at[l, pl.ds(0, 3), :, outer_cols]),)
        else:
            mid = pl.ds(middle, 128)
            moves = (
                (0, oatt.at[l, 3, :, outer_cols]),
                (1, oatt.at[l, 2 * side, :, mid]),
                (2, oatt.at[l, 1 + 2 * side, :, mid]),
            )
        for i, (b, dst) in enumerate(moves):
            n = ch + i
            far = GA.at[(l, ch) + place({**me, axis: other[axis]}) + (b,)]
            att_cp[l, "out", n] = remote(far, dst, ato_s.at[l, n], ato_r.at[l, n], peer(axis))
            att_cp[l, "own", n] = here(GA.at[(l, ch) + place(me) + (b,)], dst, atl.at[l, n])

    def att_done(l):
        for ch in range(2):
            for step in range(3):
                att_cp[l, ch, step].wait_send()
        for n in range(4):
            att_cp[l, "out", n].wait()
            att_cp[l, "own", n].wait()

    def qcols_of(l):
        A, B = SHARE[l]
        return pl.ds(pl.multiple_of((2 * me[A] + me[B]) * FQ, 128), FQ)

    def group_rows(l, i, j):
        buf = (psend, precv)[j]
        return [
            pltpu.make_async_copy(ag.at[k, i, j], buf.at[n], stsem.at[1 + j, n]) for n, k in enumerate((l, dfb_index(l)))
        ]

    def ffn_load(l):
        groups[l].ready()
        groups[dfb_index(l)].ready()
        for j in range(2):
            for cp in group_rows(l, 0, j):
                cp.start()

    def ffn_hidden(l):
        qcols = qcols_of(l)

        def pair_of_slots(i, _):
            for j in range(2):
                buf = (psend, precv)[j]
                for cp in group_rows(l, i, j):
                    cp.wait()
                wab[...] = buf[0].astype(BF16)
                wdfb[...] = buf[1].astype(BF16)

                @pl.when(i == 0)
                def _():
                    for cp in group_rows(l, 1, j):
                        cp.start()

                toks = pl.ds(pl.multiple_of((2 * i + j) * T, T), T)
                abT[:, toks] = wab[...].T
                dfbT[:, toks] = wdfb[...].T
                gu = dot(wab[...], jnp.concatenate([wi[l, 0, :, qcols], wi[l, 1, :, qcols]], axis=1))
                de = dot_t(wdfb[...], wd[l, qcols, :])
                g, u = gu[:, :FQ], gu[:, FQ:]
                act, slope_g = gelu_parts(g)
                AB[i, j, :, pl.ds(0, FQ)] = (de * u * slope_g).astype(BF16)
                AB[i, j, :, pl.ds(FQ, FQ)] = (de * act).astype(BF16)
                AB[i, j, :, pl.ds(2 * FQ, FQ)] = (act * u).astype(BF16)
            return 0

        lax.fori_loop(0, 2, pair_of_slots, 0)

    ffn_cp = {}
    kinds = (pl.ds(0, 2), pl.ds(2, 1))

    def sum_axes(l):
        return [a for a in AXES if a not in SHARE[l]]

    def ffn_block(l, i):
        (A, B), (r0, r1) = SHARE[l], sum_axes(l)
        to0, to1 = i in (0, 1), i in (0, 2)
        at0, at1 = other[r0] if to0 else me[r0], other[r1] if to1 else me[r1]
        base = at0 * weight[r0] + at1 * weight[r1]
        places = [base + i * weight[A] + j * weight[B] for i in range(2) for j in range(2)]
        for left, k, n in ((abT, 0, 2), (dfbT, 2, 1)):
            rows = jnp.concatenate([left[pl.ds(pl.multiple_of(p * R, 16), R), :] for p in places], axis=0)
            right = jnp.concatenate([AB[i, j, :, pl.ds(k * FQ, n * FQ)] for i in range(2) for j in range(2)], axis=0)
            out = dot(rows, right)
            for m in range(n):
                GF[l, at0, at1, k + m] = out[:, m * FQ:(m + 1) * FQ]
        for ch in range(2):
            if i == 0:
                ffn_send(l, ch, 0)
            elif i == (1 if FFN[l][ch][0] == r0 else 2):
                ffn_send(l, ch, 1)

    def ffn_views(l, ch):
        k = kinds[ch]
        first, second = FFN[l][ch]

        def block(at):
            return GF.at[(l,) + tuple(at[a] for a in sum_axes(l)) + (k,)]

        both, one, two = {first: other[first], second: other[second]}, {**me, first: other[first]}, {**me, second: other[second]}
        return (
            (block(both), block(two), RF1.at[l, 0, k], first),
            (block(one), block(me), RF1.at[l, 1, k], first),
            (block(two), block(me), RF2.at[l, k], second),
        )

    def ffn_send(l, ch, i):
        src, _, land, axis = ffn_views(l, ch)[i]
        ffn_cp[l, ch, i] = remote(src, land, fz_s.at[l, ch, i], fz_r.at[l, ch, i], peer(axis))

    def ffn_recv(l, ch, i):
        _, stay, land, _ = ffn_views(l, ch)[i]
        ffn_cp[l, ch, i].wait_recv()
        stay[...] = stay[...] + land[...]
        if i == 0:
            ffn_send(l, ch, 2)
        if i < 2:
            return
        dst = offn.at[l, kinds[ch], :, qcols_of(l)]
        A, B = SHARE[l]
        final = [me[a] for a in sum_axes(l)]

        def rows_of(i, j):
            return GF.at[l, final[0], final[1], kinds[ch], pl.ds(pl.multiple_of((2 * i + j) * R, 16), R), :]

        ffn_cp[l, ch, "out"] = [
            remote(rows_of(i, j), dst, fa_s.at[l, ch, n], fa_r.at[l, ch, n], to)
            for n, (i, j, to) in enumerate(
                ((me[A], other[B], peer(B)), (other[A], me[B], peer(A)), (other[A], other[B], peer(A, B)))
            )
        ]
        ffn_cp[l, ch, "own"] = here(rows_of(me[A], me[B]), dst, fl.at[l, ch])

    def ffn_done(l):
        for ch in range(2):
            for i in range(3):
                ffn_cp[l, ch, i].wait_send()
            for cp in ffn_cp[l, ch, "out"]:
                cp.wait()
            ffn_cp[l, ch, "own"].wait()

    gn_cp = {}

    def gn_send(step):
        gn_cp[step] = remote(gn, gnr.at[step], gn_s.at[step], gn_r.at[step], peer(AXES[step]))

    def gn_recv(step):
        gn_cp[step].wait()
        gn[...] = gn[...] + gnr[step]
        if step < 3:
            gn_send(step + 1)

    x_cp.wait()
    for rows in row_chunks:
        xcur[rows, :] = ab[rows, :].astype(F32)
    proj(0)
    win(0)
    out_sum(0)
    norm1(0)
    hidden(0, range(2))
    groups[0].send()
    hidden(0, range(2, F // 256))
    down_sum(0)
    norm2(0)
    proj(1)
    win(1)
    out_sum(1)
    norm1(1)
    hidden(1, range(2))
    groups[1].send()
    hidden(1, range(2, F // 256))
    cot_cp = here(cot_hbm, ab, insem.at[1])
    down_sum(1)
    pairs[0].share()
    norm2(1)
    cot_cp.wait()
    bwd_norm2(1, lambda rows: ab[rows, :].astype(F32))
    bwd_hidden(1)
    hidden_sum(1)
    pairs[1].share()
    bwd_norm1(1)
    groups[0].forward()
    dob(1)
    bwd_win(1)
    qkv_sum(1)
    att_own(1)
    groups[1].forward()
    bwd_input(1)
    bwd_norm2(0, lambda rows: xcur[rows, :])
    bwd_hidden(0)
    hidden_sum(0)
    groups[0].share()
    bwd_norm1(0)
    gn_send(0)
    dob(0)
    bwd_win(0)
    qkv_sum(0)
    bwd_input(0)
    igrad_cp = here(xcur, igrad_ref, igl.at[0])
    groups[1].share()
    groups[2].forward()
    pairs[2].share()
    att_load(1)
    att_partner(1)
    gn_recv(0)
    att_grad(1, 0)
    att_grad(1, 1)
    groups[3].forward()
    groups[2].share()
    pairs[3].share()
    ffn_load(1)
    ffn_hidden(1)
    gn_recv(1)
    groups[3].share()
    for i in range(4):
        ffn_block(1, i)
    att_load(0)
    att_own(0)
    att_partner(0)
    gn_recv(2)
    att_recv(1, 1, 0)
    att_grad(0, 0)
    att_grad(0, 1)
    groups[3].own.wait()
    ffn_load(0)
    ffn_hidden(0)
    gn_recv(3)
    att_recv(1, 0, 0)
    for i in range(4):
        ffn_block(0, i)
    ffn_recv(1, 0, 0)
    ffn_recv(1, 1, 0)
    att_recv(0, 0, 0)
    att_recv(1, 1, 1)
    att_recv(1, 0, 1)
    ffn_recv(1, 0, 1)
    ffn_recv(1, 1, 1)
    ffn_recv(0, 1, 0)
    ffn_recv(0, 0, 0)
    att_recv(0, 1, 0)
    ffn_recv(1, 1, 2)
    ffn_recv(0, 1, 1)
    att_recv(0, 0, 1)
    ffn_recv(0, 0, 1)
    ffn_recv(1, 0, 2)
    ffn_recv(0, 1, 2)
    att_recv(1, 1, 2)
    att_recv(0, 1, 1)
    att_recv(1, 0, 2)
    ffn_recv(0, 0, 2)
    att_recv(0, 0, 2)
    att_recv(0, 1, 2)

    igrad_cp.wait()
    for k in range(2 * L):
        groups[k].sent()
    for l in range(L):
        att_done(l)
        ffn_done(l)


def fused(inputs, lengths, w_qkv, w_out, w_in, w_down, norm_gain, norm_bias, cotangent):
    T, D = inputs.shape
    L, _, _, E = w_qkv.shape
    F = w_in.shape[-1]
    W, NP, NC, FQ = T // 128, E // 128, D // 256, F // GROUP
    R = D // DP
    RB = 4 * R
    vmem = pl.BlockSpec(memory_space=pltpu.VMEM)
    smem = pl.BlockSpec(memory_space=pltpu.SMEM)
    hbm = pl.BlockSpec(memory_space=pl.ANY)
    V = pltpu.VMEM
    DMA = pltpu.SemaphoreType.DMA
    scratch = [
        V((L, 3, D, E), BF16), V((L, E, D), BF16), V((L, 2, D, F), BF16), V((L, F, D), BF16),
        V((L, T, D), BF16), V((L, 3, T, E), BF16), V((L, W, NP, 128, 256), BF16), V((L, T, E), BF16),
        V((L, T, D), BF16), V((L, T, D), BF16), V((L, T, 1), F32), V((L, T, 1), F32),
        V((T, D), F32), V((T, D), F32), V((T, D), BF16),
        V((2, T, D), F32), V((2, T, D), F32),
        V((T, F), BF16), V((L, 2, T, F), BF16),
        V((2, D, 2 * T), BF16), V((2 * T, 6 * 128), BF16),
        V((D, GROUP * T), BF16), V((D, GROUP * T), BF16),
        V((2, T, D), F32), V((T, D), BF16), V((T, D), BF16), V((1 + L, 8, 128), F32),
        V((L, 2, 2, 3, RB, FQ), F32), V((L, 2, 3, RB, FQ), F32), V((L, 3, RB, FQ), F32),
        V((L, 2, 2, 2, 2, 2, 3, R, 128), F32),
        V((L, 2, 2, 2, 2, 3, R, 128), F32), V((L, 2, 2, 2, 3, R, 128), F32), V((L, 2, 2, 3, R, 128), F32),
        V((4, 4 * L, D), F32),
        DMA((L, 4)), DMA((3,)), DMA((2, NC)), DMA((2, NC)),
        DMA((2 * L,)), DMA((2 * L,)), DMA((2 * L,)), DMA((2 * L,)), DMA((2 * L,)), DMA((2 * L,)), DMA((2 * L,)),
        DMA((2 * L, 3)), DMA((2 * L, 3)),
        DMA((L,)), DMA((L,)), DMA((1,)),
        DMA((2 * L,)), DMA((2 * L,)), DMA((2 * L,)), DMA((2 * L,)), DMA((2 * L,)),
        DMA((3, 2)), DMA((L, 2, 3)), DMA((L, 2, 3)), DMA((L, 2, 3)), DMA((L, 2, 3)), DMA((L, 2)),
        DMA((L, 2, 3)), DMA((L, 2, 3)), DMA((L, 4)), DMA((L, 4)), DMA((L, 4)),
        DMA((4,)), DMA((4,)),
    ]
    outs = pl.pallas_call(
        functools.partial(kernel, T, D, E, F, L),
        out_shape=(
            jax.ShapeDtypeStruct((T, D), BF16),
            jax.ShapeDtypeStruct((T, D), F32),
            jax.ShapeDtypeStruct((L, 4, R, E), F32),
            jax.ShapeDtypeStruct((L, 3, R, F), F32),
            jax.ShapeDtypeStruct((4 * L, D), F32),
            jax.ShapeDtypeStruct((2 * L, 2, 2, T, D), F32),
            jax.ShapeDtypeStruct((2 * L, 2, T, D), F32),
        ),
        in_specs=[smem, hbm, hbm, vmem, vmem, hbm, hbm, hbm, hbm],
        out_specs=(hbm, hbm, hbm, hbm, vmem, hbm, hbm),
        scratch_shapes=scratch,
        compiler_params=pltpu.CompilerParams(collective_id=0, has_side_effects=True, vmem_limit_bytes=65400 * 2**10),
        name="encoder",
    )(lengths, inputs, cotangent, norm_gain, norm_bias, w_qkv, w_out, w_in, w_down)
    encoded, input_grad, oatt, offn, gn, _, _ = outs
    mine = lax.dynamic_slice_in_dim(gn.reshape(2, L, 2, D), lax.axis_index("dp") * R, R, axis=3)
    return (
        encoded,
        input_grad,
        oatt[:, :3],
        jnp.swapaxes(oatt[:, 3], 1, 2),
        offn[:, :2],
        jnp.swapaxes(offn[:, 2], 1, 2),
        mine[0],
        mine[1],
    )


def normalize(values, gain_vec, shift_vec):
    center = values - jnp.mean(values, -1, keepdims=True)
    spread = jnp.mean(center * center, -1, keepdims=True)
    return center * lax.rsqrt(spread + EPS) * gain_vec + shift_vec


def gating(gate_pre, up_pre):
    return jax.nn.gelu(gate_pre, approximate=False) * up_pre


def head_bias(heads_local, length):
    first_head = lax.axis_index("tensor") * heads_local
    head_order = (first_head + jnp.arange(heads_local, dtype=jnp.int32)).astype(jnp.float32)
    slopes = 2.0 ** (-8.0 * (head_order + 1.0) / HEADS)
    places = jnp.arange(length, dtype=jnp.int32)
    distance = jnp.abs(places[:, None] - places[None, :]).astype(jnp.float32)
    return -slopes[:, None, None] * distance


def scores_of(query_heads, key_heads, bias_table, key_live):
    score_scale = query_heads.shape[-1] ** (-0.5)
    raw_scores = (
        jnp.einsum("wqhe,wkhe->whqk", query_heads, key_heads, preferred_element_type=jnp.float32)
        * score_scale
        + bias_table[None]
    )
    return jnp.where(key_live[:, None, None, :], raw_scores, MASKED)


def layer_forward(layer_rows, params, bias_table, key_live):
    qkv_weight, out_weight, in_weight, down_weight, gains_now, shifts_now = params
    windows, length = key_live.shape
    heads_local = bias_table.shape[0]
    rows_low = layer_rows.astype(jnp.bfloat16)
    projected = jnp.einsum(
        "td,cde->cte", rows_low, qkv_weight, preferred_element_type=jnp.float32
    ).astype(jnp.bfloat16)
    heads_split = projected.reshape(3, windows, length, heads_local, HEAD_DIM)
    scores = scores_of(heads_split[0], heads_split[1], bias_table, key_live)
    row_max = jnp.max(scores, -1, keepdims=True)
    log_total = row_max + jnp.log(jnp.sum(jnp.exp(scores - row_max), -1, keepdims=True))
    weights_low = jnp.exp(scores - log_total).astype(jnp.bfloat16)
    mixed_heads = jnp.einsum(
        "whqk,wkhe->wqhe", weights_low, heads_split[2], preferred_element_type=jnp.float32
    )
    mixed_heads = mixed_heads.astype(jnp.bfloat16).reshape(windows * length, heads_local * HEAD_DIM)
    attended = lax.psum(
        jnp.dot(mixed_heads, out_weight, preferred_element_type=jnp.float32), "tensor"
    )
    hidden = layer_rows + attended
    normed = normalize(hidden, gains_now[0], shifts_now[0])
    normed_low = normed.astype(jnp.bfloat16)
    gate_up = jnp.einsum("td,cdf->ctf", normed_low, in_weight, preferred_element_type=jnp.float32)
    gated_low = gating(gate_up[0], gate_up[1]).astype(jnp.bfloat16)
    fed_back = lax.psum(
        jnp.dot(gated_low, down_weight, preferred_element_type=jnp.float32), "tensor"
    )
    summed = normed + fed_back
    output = normalize(summed, gains_now[1], shifts_now[1])
    stored = (
        rows_low,
        projected,
        log_total,
        mixed_heads,
        hidden,
        normed_low,
        gate_up,
        gated_low,
        summed,
    )
    return (output, stored)


def layer_backward(grad_output, stored, params, bias_table, key_live):
    rows_low, projected, log_total, mixed_heads, hidden, normed_low, gate_up, gated_low, summed = (
        stored
    )
    qkv_weight, out_weight, in_weight, down_weight, gains_now, shifts_now = params
    windows, length = key_live.shape
    heads_local = bias_table.shape[0]
    _, pull_second = jax.vjp(normalize, summed, gains_now[1], shifts_now[1])
    grad_summed, gain_second, shift_second = pull_second(grad_output)
    grad_fed = grad_summed.astype(jnp.bfloat16)
    grad_gated = jnp.einsum("td,fd->tf", grad_fed, down_weight, preferred_element_type=jnp.float32)
    grad_down = jnp.einsum("tf,td->fd", gated_low, grad_fed, preferred_element_type=jnp.float32)
    _, pull_gate = jax.vjp(gating, gate_up[0], gate_up[1])
    grad_gate_pre, grad_up_pre = pull_gate(grad_gated)
    grad_gate_up = jnp.stack([grad_gate_pre, grad_up_pre]).astype(jnp.bfloat16)
    ffn_back = lax.psum(
        jnp.einsum("ctf,cdf->td", grad_gate_up, in_weight, preferred_element_type=jnp.float32),
        "tensor",
    )
    grad_in = jnp.einsum(
        "td,ctf->cdf", normed_low, grad_gate_up, preferred_element_type=jnp.float32
    )
    grad_normed = grad_summed + ffn_back
    _, pull_first = jax.vjp(normalize, hidden, gains_now[0], shifts_now[0])
    grad_hidden, gain_first, shift_first = pull_first(grad_normed)
    grad_attended = grad_hidden.astype(jnp.bfloat16)
    grad_mixed = jnp.einsum(
        "td,ed->te", grad_attended, out_weight, preferred_element_type=jnp.float32
    ).astype(jnp.bfloat16)
    grad_out_proj = jnp.einsum(
        "te,td->ed", mixed_heads, grad_attended, preferred_element_type=jnp.float32
    )
    heads_split = projected.reshape(3, windows, length, heads_local, HEAD_DIM)
    scores = scores_of(heads_split[0], heads_split[1], bias_table, key_live)
    probabilities = jnp.exp(scores - log_total)
    probs_low = probabilities.astype(jnp.bfloat16)
    grad_heads = grad_mixed.reshape(windows, length, heads_local, HEAD_DIM)
    grad_probs = jnp.einsum(
        "wqhe,wkhe->whqk", grad_heads, heads_split[2], preferred_element_type=jnp.float32
    )
    grad_values = jnp.einsum(
        "whqk,wqhe->wkhe", probs_low, grad_heads, preferred_element_type=jnp.float32
    )
    row_dot = jnp.sum(probabilities * grad_probs, -1, keepdims=True)
    grad_scores = (probabilities * (grad_probs - row_dot)).astype(jnp.bfloat16)
    score_scale = HEAD_DIM ** (-0.5)
    grad_query = (
        jnp.einsum(
            "whqk,wkhe->wqhe", grad_scores, heads_split[1], preferred_element_type=jnp.float32
        )
        * score_scale
    )
    grad_keys = (
        jnp.einsum(
            "whqk,wqhe->wkhe", grad_scores, heads_split[0], preferred_element_type=jnp.float32
        )
        * score_scale
    )
    grad_projected = jnp.stack([grad_query, grad_keys, grad_values]).astype(jnp.bfloat16)
    grad_projected = grad_projected.reshape(3, windows * length, heads_local * HEAD_DIM)
    attn_back = lax.psum(
        jnp.einsum("cte,cde->td", grad_projected, qkv_weight, preferred_element_type=jnp.float32),
        "tensor",
    )
    grad_qkv = jnp.einsum(
        "td,cte->cde", rows_low, grad_projected, preferred_element_type=jnp.float32
    )
    grad_rows = grad_hidden + attn_back
    grad_gains = jnp.stack([gain_first, gain_second])
    grad_shifts = jnp.stack([shift_first, shift_second])
    return (grad_rows, (grad_qkv, grad_out_proj, grad_in, grad_down, grad_gains, grad_shifts))


def body(inputs, lengths, w_qkv, w_out, w_in, w_down, norm_gain, norm_bias, cotangent):
    windows = lengths.shape[0]
    length = inputs.shape[0] // windows
    heads_local = w_qkv.shape[-1] // HEAD_DIM
    bias_table = head_bias(heads_local, length)
    key_live = jnp.arange(length, dtype=jnp.int32)[None, :] < lengths[:, None]
    layers = w_qkv.shape[0]
    layer_rows = inputs.astype(jnp.float32)
    stored_all = []
    for layer_index in range(layers):
        params = (
            w_qkv[layer_index],
            w_out[layer_index],
            w_in[layer_index],
            w_down[layer_index],
            norm_gain[layer_index],
            norm_bias[layer_index],
        )
        layer_rows, stored = layer_forward(layer_rows, params, bias_table, key_live)
        stored_all.append(stored)
    encoded = layer_rows.astype(jnp.bfloat16)
    grad_rows = cotangent.astype(jnp.float32)
    pieces = [None] * layers
    for layer_index in reversed(range(layers)):
        params = (
            w_qkv[layer_index],
            w_out[layer_index],
            w_in[layer_index],
            w_down[layer_index],
            norm_gain[layer_index],
            norm_bias[layer_index],
        )
        grad_rows, layer_grads = layer_backward(
            grad_rows, stored_all[layer_index], params, bias_table, key_live
        )
        pieces[layer_index] = layer_grads
    stacked = [jnp.stack([pieces[index][member] for index in range(layers)]) for member in range(6)]
    stacked = (
        lax.psum_scatter(stacked[0], "dp", scatter_dimension=2, tiled=True),
        lax.psum_scatter(stacked[1], "dp", scatter_dimension=2, tiled=True),
        lax.psum_scatter(stacked[2], "dp", scatter_dimension=2, tiled=True),
        lax.psum_scatter(stacked[3], "dp", scatter_dimension=2, tiled=True),
        lax.psum_scatter(stacked[4], "dp", scatter_dimension=2, tiled=True),
        lax.psum_scatter(stacked[5], "dp", scatter_dimension=2, tiled=True),
    )
    return (
        encoded,
        grad_rows,
        stacked[0],
        stacked[1],
        stacked[2],
        stacked[3],
        stacked[4],
        stacked[5],
    )


def solution(mesh):
    return jax.shard_map(
        fused if mesh.shape["dp"] == DP and mesh.shape["tensor"] == 2 else body,
        mesh=mesh,
        in_specs=(
            P("dp", None),
            P("dp"),
            P(None, None, None, "tensor"),
            P(None, "tensor", None),
            P(None, None, None, "tensor"),
            P(None, "tensor", None),
            P(),
            P(),
            P("dp", None),
        ),
        out_specs=(
            P("dp", None),
            P("dp", None),
            P(None, None, "dp", "tensor"),
            P(None, "tensor", "dp"),
            P(None, None, "dp", "tensor"),
            P(None, "tensor", "dp"),
            P(None, None, "dp"),
            P(None, None, "dp"),
        ),
        check_vma=False,
    )
```
